512 devices in a mesh: rel: 8 (over y), dom: 64 (over z, x, core).
Axes of the slice: x: 4, y: 8, z: 8, core: 2. Of those that a mesh axis runs over, the one named last changes fastest.
Arguments:
- node_feats: bfloat16 [16384, 1024], P('dom'), may hold values from -6 to 6
- rel_weight: bfloat16 [8, 1024, 1024], P('rel'), may hold values from -0.1875 to 0.1875
- att_src: float32 [8, 1024], P('rel')
- att_dst: float32 [8, 1024], P('rel')
- src_row: int32 [8, 64, 64, 16], P('rel', 'dom'), may hold values from 0 to 255, as said below
- dst_row: int32 [8, 64, 64, 16], P('rel', 'dom'), may hold values from -1 to 255, as said below
Outputs:
- aggregated: bfloat16 [16384, 1024], P('dom', 'rel')
The draws below stay inside these ranges and needn't reach their ends.
Inputs may be any that keep to these rules, and one draw needn't show every extreme that they name: Slot k of the pair (p, q) describes the same edge in src_row[r, p, q, k] and dst_row[r, q, p, k]. Each pair's live slots come first; each pair has 1 to 16 edges, and in every relation some target partition receives 16 edges from every source partition. Source rows of empty slots are arbitrary valid rows. `dst_row`: -1 marks an empty slot.
All inputs are finite; a program needn't handle non-finite values.
Results may differ from the reference program's by a relative error of at most 0.015.
Values may be sent and summed in bfloat16 or wider, within the bound.
A program may use at most 64 MiB of HBM per device.

```python
import jax
import jax.numpy as jnp
from jax import lax

D = 1024
HEADS = 4
NODE_DEV = 256
CAP = 16
REL = 8
NODES = 16384
N_DOM = 64


def edge_table(key):
    counts = jax.random.randint(jax.random.fold_in(key, 1), (REL, N_DOM, N_DOM), 1, CAP + 1)
    full_target = jax.random.randint(jax.random.fold_in(key, 2), (REL,), 0, N_DOM)
    counts = jnp.where(jnp.arange(N_DOM)[None, None, :] == full_target[:, None, None], CAP, counts)
    is_valid = jnp.arange(CAP)[None, None, None, :] < counts[..., None]
    sources = jax.random.randint(jax.random.fold_in(key, 3), (REL, N_DOM, N_DOM, CAP), 0, NODE_DEV)
    base_rows = jax.random.randint(jax.random.fold_in(key, 4), (REL, N_DOM, N_DOM, CAP), 0, NODE_DEV)
    shifts = jax.random.randint(jax.random.fold_in(key, 5), (REL, N_DOM, N_DOM, CAP), 0, 3)
    targets = jnp.right_shift(base_rows, shifts)
    targets = jnp.where(is_valid, targets, -1)
    return (sources.astype(jnp.int32), targets.astype(jnp.int32))


def draw_src_row(key, part):
    sources, targets = edge_table(key)
    return sources


def draw_dst_row(key, part):
    sources, targets = edge_table(key)
    return jnp.transpose(targets, (0, 2, 1, 3))


def draw_att_src(key, part):
    key = jax.random.fold_in(key, 21)
    return jax.random.normal(key, (REL, D), jnp.float32) * 0.15


def draw_att_dst(key, part):
    key = jax.random.fold_in(key, 22)
    return jax.random.normal(key, (REL, D), jnp.float32) * 0.15


def steps_of(rng, shape, pieces, smallest, largest):
    loudness = 1.0
    for dim, shards_of in pieces:
        heights = jax.random.uniform(jax.random.fold_in(jax.random.fold_in(rng, 6), dim), (shards_of,), jnp.float32, smallest / len(pieces), largest / len(pieces))
        loudness = loudness * jnp.repeat(jnp.exp(heights), shape[dim] // shards_of).reshape((-1,) + (1,) * (len(shape) - 1 - dim))
    return loudness


def bell_draw(stream_key, dims, scale, reach, pieces=(), dtype=jnp.bfloat16):
    gain = steps_of(stream_key, dims, pieces, -0.22, 0.18) if pieces else 1.0
    array = jax.random.normal(stream_key, dims, jnp.float32) * scale * gain
    return jnp.minimum(jnp.maximum(array, -reach), reach).astype(dtype)


def setup_inputs(seed: int = 0) -> dict:
    key_of = jax.random.split(jax.random.key(seed), 7)
    node_feats = bell_draw(key_of[0], (NODES, D), 1.0, 6.0, ((0, 64),))
    rel_weight = bell_draw(key_of[1], (REL, D, D), D ** -0.5, 0.1875, ((0, 8),))
    att_src = draw_att_src(jax.random.fold_in(key_of[6], 71), 0)
    att_dst = draw_att_dst(jax.random.fold_in(key_of[6], 71), 0)
    src_row = draw_src_row(jax.random.fold_in(key_of[6], 71), 0)
    dst_row = draw_dst_row(jax.random.fold_in(key_of[6], 71), 0)
    return dict(node_feats=node_feats, rel_weight=rel_weight, att_src=att_src, att_dst=att_dst, src_row=src_row, dst_row=dst_row)


def head_matrix(vector):
    width = vector.shape[0]
    mask = (jnp.arange(width) // (width // HEADS))[:, None] == jnp.arange(HEADS)[None, :]
    return jnp.where(mask, vector[:, None], jnp.zeros((), jnp.float32))


def reference(node_feats, rel_weight, att_src, att_dst, src_row, dst_row):
    total_out = jnp.zeros((NODES, D), jnp.float32)
    offsets = jnp.arange(N_DOM).astype(jnp.int32) * NODE_DEV
    for relation in range(REL):
        proj = jnp.dot(node_feats, rel_weight[relation], preferred_element_type=jnp.float32).astype(jnp.bfloat16)
        proj_f = proj.astype(jnp.float32)
        src_all = jnp.dot(proj_f, head_matrix(att_src[relation]), precision=lax.Precision.HIGHEST)
        dst_all = jnp.dot(proj_f, head_matrix(att_dst[relation]), precision=lax.Precision.HIGHEST)
        src_glob = (src_row[relation] + offsets[:, None, None]).reshape(-1).astype(jnp.int32)
        dst_local = jnp.transpose(dst_row[relation], (1, 0, 2))
        is_valid = (dst_local >= 0).reshape(-1)
        dst_glob = (dst_local + offsets[None, :, None]).reshape(-1).astype(jnp.int32)
        segment = jnp.where(is_valid, dst_glob, NODES).astype(jnp.int32)
        clipped = jnp.minimum(segment, NODES - 1)
        score = jax.nn.leaky_relu(src_all[src_glob] + dst_all[clipped], 0.2)
        score = jnp.where(is_valid[:, None], score, jnp.float32(-1e30))
        peak_score = jax.ops.segment_max(score, segment, NODES + 1)
        expo = jnp.where(is_valid[:, None], jnp.exp(score - peak_score[segment]), jnp.float32(0.0))
        seg_total = jax.ops.segment_sum(expo, segment, NODES + 1)
        attn_weight = expo / jnp.where(is_valid[:, None], seg_total[segment], jnp.float32(1.0))
        rows_f = proj_f[src_glob].reshape(-1, HEADS, D // HEADS)
        message = (rows_f * attn_weight[:, :, None]).reshape(-1, D).astype(jnp.bfloat16)
        rel_out = jax.ops.segment_sum(message.astype(jnp.float32), segment, NODES + 1)[:NODES]
        rounded = lax.optimization_barrier(rel_out.astype(jnp.bfloat16))
        total_out = total_out + rounded.astype(jnp.float32)
    return total_out.astype(jnp.bfloat16)
```

```python
import jax
import jax.numpy as jnp
from jax import lax
from jax.experimental import pallas as pl
from jax.experimental.pallas import tpu as pltpu
from jax.sharding import PartitionSpec as P

MESH = pl.DeviceIdType.MESH
HEADS = 4
N = 256
D = 1024
CB = 128
G = 8
ZN = 8
RN = 8
F32 = jnp.float32
BF = jnp.bfloat16
ORDER = (0, 1, 7, 2, 6, 3, 5, 4)
TO_RIGHT = (0, 7, 2, 5)


def split3(v):
    hi = v.astype(BF).astype(F32)
    rest = v - hi
    mid = rest.astype(BF).astype(F32)
    low = rest - mid
    return jnp.concatenate([hi, mid, low, jnp.zeros_like(v)], axis=0).astype(BF)


def join3(v):
    return v[0:8] + v[8:16] + v[16:24]


def leaky(v):
    return jnp.where(v >= 0, v, 0.2 * v)


def dot(a, b):
    return jnp.dot(a, b, preferred_element_type=F32)


def dot_nt(a, b):
    return lax.dot_general(a, b, (((1,), (1,)), ((), ())), preferred_element_type=F32)


def block_transpose(tiles):
    lane_block = lax.broadcasted_iota(jnp.int32, (8, 128), 1) // 16
    for bit in (1, 2, 4):
        low = (lane_block & bit) == 0
        out = list(tiles)
        for i in range(8):
            if i & bit:
                continue
            first, second = tiles[i], tiles[i + bit]
            out[i] = jnp.where(low, first, pltpu.roll(second, 16 * bit, 1))
            out[i + bit] = jnp.where(low, pltpu.roll(first, 128 - 16 * bit, 1), second)
        tiles = out
    return tiles


def kernel(
    feat_ref, w_ref, asrc_ref, adst_ref, src_ref, dst_ref, out_ref,
    x_buf, w_buf, proj, pall, onehot, picked,
    idx_send, idx_recv, idx_rows, idx_all,
    s1, r1, s2, r2, s3, r3, al_send, al_all,
    max_cols, dst_hot, expo,
    zs_r, zs_l, zr_r, zr_l,
    in_sem, y_ss, y_rs, x_ss, x_rs, g_ss, g_rs, h_ss, h_rs, k_ss, k_rs, m_ss, m_rs, n_ss, n_rs, o_ss, o_rs, z_ss, z_rs,
):
    r = lax.axis_index("rel")
    p = lax.axis_index("dom")
    z, g = p // G, p % G
    x, a = g // 2, g % 2
    load_x = pltpu.make_async_copy(feat_ref, x_buf, in_sem.at[0])
    load_w = pltpu.make_async_copy(w_ref, w_buf, in_sem.at[1])
    load_x.start()
    load_w.start()

    def in_group(i):
        return (r, z * G + i)

    def in_z(i):
        return (r, i * G + g)

    def in_rel(i):
        return (i, p)

    def hop(i, amount, size):
        return lax.rem(i + amount + size, size)

    barrier = pltpu.get_barrier_semaphore()
    for d in range(1, 8):
        for dev in (in_group(hop(g, d, G)), in_z(hop(z, d, ZN)), in_rel(hop(r, d, RN))):
            pl.semaphore_signal(barrier, inc=1, device_id=dev, device_id_type=MESH)
    pl.semaphore_wait(barrier, 21)

    sent = []

    def copy(src, dst, ss, rs, dev):
        return pltpu.make_async_remote_copy(
            src_ref=src, dst_ref=dst, send_sem=ss, recv_sem=rs, device_id=dev, device_id_type=MESH
        )

    def send(*args):
        c = copy(*args)
        c.start()
        sent.append(c)

    def exchange(sbuf, rbuf, ss, rs, me, member):
        rbuf[me] = sbuf[me]
        for d in range(1, 8):
            to = hop(me, d, 8)
            send(sbuf.at[to], rbuf.at[me], ss.at[d], rs.at[8 - d], member(to))

    def arrived(sbuf, rbuf, ss, rs, me, member):
        for d in range(1, 8):
            frm = hop(me, d, 8)
            copy(sbuf.at[frm], rbuf.at[frm], ss.at[d], rs.at[d], member(frm)).wait_recv()

    src_f = src_ref[...].astype(F32)
    for i in range(G):
        idx_send[i] = jnp.broadcast_to(src_f[i : i + 1], (8, 128))
    exchange(idx_send, idx_recv, g_ss, g_rs, g, in_group)

    load_x.wait()
    load_w.wait()
    feats = x_buf[...]
    for i in range(4):
        part = dot(feats, w_buf[:, 256 * i : 256 * (i + 1)]).astype(BF)
        proj[2 * i] = part[:, :CB]
        proj[2 * i + 1] = part[:, CB:]

    arrived(idx_send, idx_recv, g_ss, g_rs, g, in_group)
    for i in range(G):
        idx_rows[i : i + 1, :] = idx_recv[i, 0:1, :]
    idx_all[0] = idx_rows[...]
    for d in range(1, 8):
        send(idx_rows, idx_all.at[8 - d], h_ss.at[d], h_rs.at[8 - d], in_rel(hop(r, d, RN)))

    pall[g, 0] = proj[r]
    for d in ORDER[1:]:
        to = hop(r, d, RN)
        send(proj.at[to], pall.at[g, 8 - d], y_ss.at[d], y_rs.at[8 - d], in_rel(to))

    x_r, x_l, x_2 = hop(x, 1, 4), hop(x, 3, 4), hop(x, 2, 4)
    g_r, g_l, g_2 = 2 * x_r + a, 2 * x_l + a, 2 * x_2 + a
    partner = 2 * x + 1 - a

    def give(kind, j, owner, to):
        send(pall.at[owner, j], pall.at[owner, j], x_ss.at[kind, j], x_rs.at[kind, j], in_group(to))

    def got(kind, j, owner):
        copy(pall.at[owner, j], pall.at[owner, j], x_ss.at[kind, j], x_rs.at[kind, j], in_group(partner)).wait_recv()

    def stage_own(j):
        if j:
            copy(proj.at[0], pall.at[g, j], y_ss.at[j], y_rs.at[j], in_rel(hop(r, j, RN))).wait_recv()
        give(0, j, g, g_r)
        give(1, j, g, g_l)
        give(3, j, g, partner)

    def stage_near(j):
        got(0, j, g_l)
        if j in TO_RIGHT:
            give(2, j, g_l, g_r)
        give(4, j, g_l, partner)
        got(1, j, g_r)
        if j not in TO_RIGHT:
            give(2, j, g_r, g_l)
        give(5, j, g_r, partner)

    def stage_far(j):
        got(2, j, g_2)
        give(6, j, g_2, partner)

    def stage_pick(j):
        got(3, j, partner)
        got(4, j, 2 * x_l + 1 - a)
        got(5, j, 2 * x_r + 1 - a)
        got(6, j, 2 * x_2 + 1 - a)

        def body(i, carry):
            rows = dot(onehot[j, i], pall[i, j]).astype(BF)
            picked[:, pl.ds(pl.multiple_of(j * 128 + i * 16, 16), 16), :] = rows.reshape(ZN, 16, CB)
            return carry

        lax.fori_loop(0, G, body, 0)

    stage_own(0)

    row8 = lax.broadcasted_iota(jnp.int32, (8, D), 0)
    lane8 = lax.broadcasted_iota(jnp.int32, (8, D), 1)
    att = jnp.where(row8 < HEADS, asrc_ref[...], adst_ref[...])
    att = split3(jnp.where(lane8 // (D // HEADS) == row8 % HEADS, att, 0.0))
    total = jnp.zeros((32, N), F32)
    for c in range(RN):
        total = total + dot_nt(att[:, CB * c : CB * (c + 1)], proj[c])
    score = join3(total)
    score3 = split3(score)

    iota_n = lax.broadcasted_iota(jnp.int32, (N, 128), 0)
    src_i = src_ref[...]
    for i in range(G):
        hot = jnp.where(src_i[i : i + 1] == iota_n, 1.0, 0.0).astype(BF)
        s1[i] = join3(dot(score3, hot))
    exchange(s1, r1, k_ss, k_rs, g, in_group)

    stage_own(1)

    arrived(s1, r1, k_ss, k_rs, g, in_group)
    for i, tile in enumerate(block_transpose([r1[i] for i in range(G)])):
        s2[i] = tile
    exchange(s2, r2, m_ss, m_rs, z, in_z)

    stage_own(7)
    stage_near(0)

    for d in range(1, 8):
        copy(idx_rows, idx_all.at[d], h_ss.at[d], h_rs.at[d], in_rel(hop(r, d, RN))).wait_recv()
    iota_l = lax.broadcasted_iota(jnp.int32, (128, N), 1).astype(F32)

    def hot_body(j, carry):
        cols = idx_all[j].T
        for i in range(G):
            onehot[j, i] = jnp.where(cols[:, i : i + 1] == iota_l, 1.0, 0.0).astype(BF)
        return carry

    lax.fori_loop(0, RN, hot_body, 0)

    arrived(s2, r2, m_ss, m_rs, z, in_z)
    row = lax.broadcasted_iota(jnp.int32, (8, 128), 0)
    lane = lax.broadcasted_iota(jnp.int32, (64, 128), 1)
    neg = -jnp.inf

    def max_body(t, carry):
        base = pl.multiple_of(t * 64, 64)
        iota_t = lax.broadcasted_iota(jnp.int32, (64, 128), 0) + base
        best = [jnp.full((64, 128), neg, F32) for _ in range(HEADS)]
        for i in range(ZN):
            mask = dst_ref[i : i + 1, :] == iota_t
            dst_hot[i, pl.ds(base, 64), :] = jnp.where(mask, 1.0, 0.0).astype(BF)
            for h in range(HEADS):
                best[h] = jnp.maximum(best[h], jnp.where(mask, r2[i, h : h + 1, :], neg))
        cols = jnp.zeros((64, 128), F32)
        for h in range(HEADS):
            cols = jnp.where(lane == h, jnp.max(best[h], axis=1, keepdims=True), cols)
        max_cols[pl.ds(base, 64), :] = cols
        return carry

    lax.fori_loop(0, 4, max_body, 0)
    peak_src = max_cols[...].T[0:8]
    row_n = lax.broadcasted_iota(jnp.int32, (8, N), 0)
    dst_up = pltpu.roll(score, 4, 0)
    peak = jnp.where(peak_src == neg, 0.0, leaky(peak_src + dst_up))
    table = split3(jnp.where(row_n < HEADS, peak, score))
    seg = jnp.zeros((32, N), F32)
    for i in range(ZN):
        near = join3(dot(table, dst_hot[i]))
        edge = leaky(r2[i] + pltpu.roll(near, 4, 0))
        live = (row < HEADS) & (dst_ref[i : i + 1, :] >= 0)
        e = jnp.where(live, jnp.exp(jnp.where(live, edge - near, 0.0)), 0.0)
        expo[i] = e
        seg = seg + dot_nt(split3(e), dst_hot[i])
    seg3 = split3(join3(seg))
    for i in range(ZN):
        live = (row < HEADS) & (dst_ref[i : i + 1, :] >= 0)
        under = jnp.where(live, join3(dot(seg3, dst_hot[i])), 1.0)
        alpha = jnp.where(live, expo[i] / under, 0.0)
        s3[i] = jnp.where(row == HEADS, dst_ref[i : i + 1, :].astype(F32), alpha)
    exchange(s3, r3, n_ss, n_rs, z, in_z)

    stage_own(2)
    stage_near(1)
    stage_own(6)

    arrived(s3, r3, n_ss, n_rs, z, in_z)
    for h in range(HEADS):
        al_send[h, 0:8] = r3[:, h, :]
        al_send[h, 8:16] = r3[:, HEADS, :]
    al_all[0] = al_send[r // 2]
    for d in range(1, 8):
        to = hop(r, d, RN)
        send(al_send.at[to // 2], al_all.at[8 - d], o_ss.at[d], o_rs.at[8 - d], in_rel(to))

    stage_near(7)
    stage_far(0)
    stage_own(3)
    stage_near(2)
    stage_far(1)
    stage_own(5)
    stage_pick(0)
    stage_near(6)
    stage_far(7)
    stage_own(4)
    stage_pick(1)
    stage_near(3)
    stage_far(2)
    stage_pick(7)
    stage_near(5)
    stage_far(6)
    stage_pick(2)
    stage_near(4)
    stage_far(3)
    stage_pick(6)
    stage_far(5)
    stage_pick(3)
    stage_far(4)
    stage_pick(5)
    stage_pick(4)

    for d in range(1, 8):
        copy(al_send.at[0], al_all.at[d], o_ss.at[d], o_rs.at[d], in_rel(hop(r, d, RN))).wait_recv()

    def part(zt):
        acc = jnp.zeros((N, CB), F32)
        for j in range(0, RN, 2):
            both = []
            for jj in (j, j + 1):
                alpha = al_all[jj, pl.ds(zt, 1), :]
                target = al_all[jj, pl.ds(zt + 8, 1), :]
                both.append(jnp.where(target == iota_n.astype(F32), alpha, 0.0).astype(BF))
            acc = acc + dot(jnp.concatenate(both, axis=1), picked[zt, j * 128 : j * 128 + 256, :])
        return acc

    right, left = in_z(hop(z, 1, ZN)), in_z(hop(z, -1, ZN))
    half = N // 2

    def ring(way, s, dev):
        sbuf, rbuf = (zs_r, zr_r) if way == 0 else (zs_l, zr_l)
        rows = pl.ds(half * way, half) if s == 0 else pl.ds(0, N)
        return copy(sbuf.at[s, rows], rbuf.at[s, rows], z_ss.at[way, s], z_rs.at[way, s], dev)

    def ring_send(way, s, dev):
        c = ring(way, s, dev)
        c.start()
        sent.append(c)

    far = part(hop(z, 4, ZN)).astype(BF)
    zs_r[0, 0:half] = far[0:half]
    ring_send(0, 0, right)
    zs_l[0, half:N] = far[half:N]
    ring_send(1, 0, left)
    for s in (1, 2, 3):
        mine_r = part(hop(z, 4 - s, ZN))
        mine_l = part(hop(z, s - 4, ZN))
        for way, mine, dev in ((0, mine_r, right), (1, mine_l, left)):
            sbuf, rbuf = (zs_r, zr_r) if way == 0 else (zs_l, zr_l)
            ring(way, s - 1, dev).wait_recv()
            if s == 1:
                zs = slice(half * way, half * (way + 1))
                other = slice(half * (1 - way), half * (2 - way))
                sbuf[s, zs] = (mine[zs] + rbuf[0, zs].astype(F32)).astype(BF)
                sbuf[s, other] = mine[other].astype(BF)
            else:
                sbuf[s] = (mine + rbuf[s - 1].astype(F32)).astype(BF)
            ring_send(way, s, dev)
    own = part(z)
    ring(0, 3, right).wait_recv()
    ring(1, 3, left).wait_recv()
    out_ref[...] = (own + zr_r[3].astype(F32) + zr_l[3].astype(F32)).astype(BF)
    for c in sent:
        c.wait_send()


def on_device(node_feats, rel_weight, att_src, att_dst, src_row, dst_row):
    src = src_row.reshape(ZN, G, 16).transpose(1, 0, 2).reshape(G, 128)
    dst = dst_row.reshape(ZN, 128)
    vmem = pl.BlockSpec(memory_space=pltpu.VMEM)
    hbm = pl.BlockSpec(memory_space=pl.ANY)
    tile8 = pltpu.VMEM((8, 8, 128), F32)
    dma = pltpu.SemaphoreType.DMA
    return pl.pallas_call(
        kernel,
        out_shape=jax.ShapeDtypeStruct((N, CB), BF),
        in_specs=[hbm, hbm, vmem, vmem, vmem, vmem],
        out_specs=vmem,
        scratch_shapes=[
            pltpu.VMEM((N, D), BF),
            pltpu.VMEM((D, D), BF),
            pltpu.VMEM((RN, N, CB), BF),
            pltpu.VMEM((G, RN, N, CB), BF),
            pltpu.VMEM((RN, G, 128, N), BF),
            pltpu.VMEM((ZN, D, CB), BF),
            tile8, tile8,
            pltpu.VMEM((8, 128), F32),
            tile8,
            tile8, tile8, tile8, tile8, tile8, tile8,
            pltpu.VMEM((HEADS, 16, 128), F32),
            pltpu.VMEM((RN, 16, 128), F32),
            pltpu.VMEM((N, 128), F32),
            pltpu.VMEM((ZN, N, 128), BF),
            tile8,
            pltpu.VMEM((4, N, CB), BF),
            pltpu.VMEM((4, N, CB), BF),
            pltpu.VMEM((4, N, CB), BF),
            pltpu.VMEM((4, N, CB), BF),
            dma((2,)),
            dma((8,)), dma((8,)),
            dma((7, 8)), dma((7, 8)),
            dma((8,)), dma((8,)),
            dma((8,)), dma((8,)),
            dma((8,)), dma((8,)),
            dma((8,)), dma((8,)),
            dma((8,)), dma((8,)),
            dma((8,)), dma((8,)),
            dma((2, 4)), dma((2, 4)),
        ],
        compiler_params=pltpu.CompilerParams(
            collective_id=0, has_side_effects=True, vmem_limit_bytes=48 * 1024 * 1024
        ),
    )(node_feats, rel_weight[0], att_src, att_dst, src, dst)


def solution(mesh):
    placed = (
        P("dom", None),
        P("rel", None, None),
        P("rel", None),
        P("rel", None),
        P("rel", "dom", None, None),
        P("rel", "dom", None, None),
    )
    return jax.shard_map(
        on_device, mesh=mesh, in_specs=placed, out_specs=P("dom", "rel"), check_vma=False
    )
```

```python
import jax
import jax.numpy as jnp
from jax import lax
from jax.experimental import pallas as pl
from jax.experimental.pallas import tpu as pltpu
from jax.sharding import PartitionSpec as P

MESH = pl.DeviceIdType.MESH
HEADS = 4
N = 256
D = 1024
CB = 128
G = 8
ZN = 8
RN = 8
F32 = jnp.float32
BF = jnp.bfloat16
ORDER = (0, 1, 7, 2, 6, 3, 5, 4)
TO_RIGHT = (0, 7, 2, 5)


def split3(v):
    hi = v.astype(BF).astype(F32)
    rest = v - hi
    mid = rest.astype(BF).astype(F32)
    low = rest - mid
    return jnp.concatenate([hi, mid, low, jnp.zeros_like(v)], axis=0).astype(BF)


def join3(v):
    return v[0:8] + v[8:16] + v[16:24]


def leaky(v):
    return jnp.where(v >= 0, v, 0.2 * v)


def dot(a, b):
    return jnp.dot(a, b, preferred_element_type=F32)


def dot_nt(a, b):
    return lax.dot_general(a, b, (((1,), (1,)), ((), ())), preferred_element_type=F32)


def block_transpose(tiles):
    lane_block = lax.broadcasted_iota(jnp.int32, (8, 128), 1) // 16
    for bit in (1, 2, 4):
        low = (lane_block & bit) == 0
        out = list(tiles)
        for i in range(8):
            if i & bit:
                continue
            first, second = tiles[i], tiles[i + bit]
            out[i] = jnp.where(low, first, pltpu.roll(second, 16 * bit, 1))
            out[i + bit] = jnp.where(low, pltpu.roll(first, 128 - 16 * bit, 1), second)
        tiles = out
    return tiles


def kernel(
    feat_ref, w_ref, asrc_hbm, adst_hbm, src_hbm, dst_hbm, out_ref,
    x_buf, w_buf, asrc_ref, adst_ref, src_raw, dst_raw, src_ref, dst_ref, spread, proj, pall, onehot, picked,
    idx_send, idx_recv, idx_rows, idx_all,
    s1, r1, s2, r2, s3, r3, al_send, al_all,
    max_cols, dst_hot, expo,
    zs, zr,
    in_sem, y_ss, y_rs, x_ss, x_rs, g_ss, g_rs, h_ss, h_rs, k_ss, k_rs, m_ss, m_rs, n_ss, n_rs, o_ss, o_rs, z_ss, z_rs,
):
    r = lax.axis_index("rel")
    p = lax.axis_index("dom")
    z, g = p // G, p % G
    x, a = g // 2, g % 2
    load_x = pltpu.make_async_copy(feat_ref, x_buf, in_sem.at[0])
    load_w = pltpu.make_async_copy(w_ref, w_buf, in_sem.at[1])
    load_src = pltpu.make_async_copy(src_hbm, src_raw, in_sem.at[2])
    load_dst = pltpu.make_async_copy(dst_hbm, dst_raw, in_sem.at[3])
    load_as = pltpu.make_async_copy(asrc_hbm, asrc_ref, in_sem.at[4])
    load_ad = pltpu.make_async_copy(adst_hbm, adst_ref, in_sem.at[5])
    for load in (load_src, load_dst, load_x, load_w, load_as, load_ad):
        load.start()

    def in_group(i):
        return (r, z * G + i)

    def in_z(i):
        return (r, i * G + g)

    def in_rel(i):
        return (i, p)

    def hop(i, amount, size):
        return lax.rem(i + amount + size, size)

    barrier = pltpu.get_barrier_semaphore()
    for d in range(1, 8):
        for dev in (in_group(hop(g, d, G)), in_z(hop(z, d, ZN)), in_rel(hop(r, d, RN))):
            pl.semaphore_signal(barrier, inc=1, device_id=dev, device_id_type=MESH)

    lane_block = lax.broadcasted_iota(jnp.int32, (8, 128), 1) // 16
    load_src.wait()
    spread[...] = jnp.concatenate([src_raw[...].astype(F32)] * 8, axis=0).T
    src_f = jnp.zeros((8, 128), F32)
    for i in range(ZN):
        src_f = jnp.where(lane_block == i, spread[8 * i : 8 * i + 8, :], src_f)
    src_ref[...] = src_f.astype(jnp.int32)
    load_dst.wait()
    spread[...] = jnp.concatenate([dst_raw[...].astype(F32)] * 8, axis=0).T
    dst_f = jnp.zeros((8, 128), F32)
    for i in range(G):
        dst_f = jnp.where(lane_block == i, spread[pl.ds(i, 8, stride=8), :], dst_f)
    dst_ref[...] = dst_f.astype(jnp.int32)
    idx_rows[...] = src_f
    idx_all[0] = src_f

    pl.semaphore_wait(barrier, 21)

    sent = []

    def copy(src, dst, ss, rs, dev):
        return pltpu.make_async_remote_copy(
            src_ref=src, dst_ref=dst, send_sem=ss, recv_sem=rs, device_id=dev, device_id_type=MESH
        )

    def send(*args):
        c = copy(*args)
        c.start()
        sent.append(c)

    def exchange(sbuf, rbuf, ss, rs, me, member):
        rbuf[me] = sbuf[me]
        for d in ORDER[:0:-1]:
            to = hop(me, d, 8)
            send(sbuf.at[to], rbuf.at[me], ss.at[d], rs.at[8 - d], member(to))

    def arrived(sbuf, rbuf, ss, rs, me, member):
        for d in range(1, 8):
            frm = hop(me, d, 8)
            copy(sbuf.at[frm], rbuf.at[frm], ss.at[d], rs.at[d], member(frm)).wait_recv()

    for d in ORDER[:0:-1]:
        send(idx_rows, idx_all.at[8 - d], h_ss.at[d], h_rs.at[8 - d], in_rel(hop(r, d, RN)))

    load_x.wait()
    load_w.wait()
    feats = x_buf[...]
    for i in range(4):
        part = dot(feats, w_buf[:, 256 * i : 256 * (i + 1)]).astype(BF)
        proj[2 * i] = part[:, :CB]
        proj[2 * i + 1] = part[:, CB:]

    pall[g, 0] = proj[r]
    for d in ORDER[1:]:
        to = hop(r, d, RN)
        send(proj.at[to], pall.at[g, 8 - d], y_ss.at[d], y_rs.at[8 - d], in_rel(to))

    x_r, x_l, x_2 = hop(x, 1, 4), hop(x, 3, 4), hop(x, 2, 4)
    g_r, g_l, g_2 = 2 * x_r + a, 2 * x_l + a, 2 * x_2 + a
    partner = 2 * x + 1 - a

    def give(kind, j, owner, to):
        send(pall.at[owner, j], pall.at[owner, j], x_ss.at[kind, j], x_rs.at[kind, j], in_group(to))

    def got(kind, j, owner):
        copy(pall.at[owner, j], pall.at[owner, j], x_ss.at[kind, j], x_rs.at[kind, j], in_group(partner)).wait_recv()

    def stage_own(j):
        if j:
            copy(proj.at[0], pall.at[g, j], y_ss.at[j], y_rs.at[j], in_rel(hop(r, j, RN))).wait_recv()
        give(0, j, g, g_r)
        give(1, j, g, g_l)
        give(3, j, g, partner)

    def stage_near(j):
        got(0, j, g_l)
        if j in TO_RIGHT:
            give(2, j, g_l, g_r)
        give(4, j, g_l, partner)
        got(1, j, g_r)
        if j not in TO_RIGHT:
            give(2, j, g_r, g_l)
        give(5, j, g_r, partner)

    def stage_far(j):
        got(2, j, g_2)
        give(6, j, g_2, partner)

    def stage_pick(j):
        got(3, j, partner)
        got(4, j, 2 * x_l + 1 - a)
        got(5, j, 2 * x_r + 1 - a)
        got(6, j, 2 * x_2 + 1 - a)

        for i in range(G):
            rows = dot(onehot[j, i], pall[i, j]).astype(BF)
            k = j * 128 + i * 16
            picked[:, k : k + 16, :] = rows.reshape(ZN, 16, CB)

    stage_own(0)

    load_as.wait()
    load_ad.wait()
    row8 = lax.broadcasted_iota(jnp.int32, (8, D), 0)
    lane8 = lax.broadcasted_iota(jnp.int32, (8, D), 1)
    att = jnp.where(row8 < HEADS, asrc_ref[...], adst_ref[...])
    att = split3(jnp.where(lane8 // (D // HEADS) == row8 % HEADS, att, 0.0))
    total = jnp.zeros((32, N), F32)
    for c in range(RN):
        total = total + dot_nt(att[:, CB * c : CB * (c + 1)], proj[c])
    score = join3(total)
    score3 = split3(score)

    iota_n = lax.broadcasted_iota(jnp.int32, (N, 128), 0)
    src_i = src_ref[...]
    for i in range(G):
        hot = jnp.where(src_i[i : i + 1] == iota_n, 1.0, 0.0).astype(BF)
        s1[i] = join3(dot(score3, hot))
    exchange(s1, r1, k_ss, k_rs, g, in_group)

    for d in range(1, 8):
        copy(idx_rows, idx_all.at[d], h_ss.at[d], h_rs.at[d], in_rel(hop(r, d, RN))).wait_recv()
    for i in range(G):
        idx_send[i] = idx_all[:, i, :]
    exchange(idx_send, idx_recv, g_ss, g_rs, g, in_group)

    stage_own(1)
    stage_own(7)

    arrived(s1, r1, k_ss, k_rs, g, in_group)
    for i, tile in enumerate(block_transpose([r1[i] for i in range(G)])):
        s2[i] = tile
    exchange(s2, r2, m_ss, m_rs, z, in_z)

    stage_near(0)
    stage_own(2)
    stage_own(6)
    stage_near(1)
    stage_near(7)

    arrived(idx_send, idx_recv, g_ss, g_rs, g, in_group)
    iota_l = lax.broadcasted_iota(jnp.int32, (128, N), 1).astype(F32)

    def hot_body(i, carry):
        cols = idx_recv[i].T
        for j in range(RN):
            onehot[j, i] = jnp.where(cols[:, j : j + 1] == iota_l, 1.0, 0.0).astype(BF)
        return carry

    lax.fori_loop(0, G, hot_body, 0)

    arrived(s2, r2, m_ss, m_rs, z, in_z)
    row = lax.broadcasted_iota(jnp.int32, (8, 128), 0)
    lane = lax.broadcasted_iota(jnp.int32, (64, 128), 1)
    neg = -jnp.inf

    def max_body(t, carry):
        base = pl.multiple_of(t * 64, 64)
        iota_t = lax.broadcasted_iota(jnp.int32, (64, 128), 0) + base
        best = [jnp.full((64, 128), neg, F32) for _ in range(HEADS)]
        for i in range(ZN):
            mask = dst_ref[i : i + 1, :] == iota_t
            dst_hot[i, pl.ds(base, 64), :] = jnp.where(mask, 1.0, 0.0).astype(BF)
            for h in range(HEADS):
                best[h] = jnp.maximum(best[h], jnp.where(mask, r2[i, h : h + 1, :], neg))
        cols = jnp.zeros((64, 128), F32)
        for h in range(HEADS):
            cols = jnp.where(lane == h, jnp.max(best[h], axis=1, keepdims=True), cols)
        max_cols[pl.ds(base, 64), :] = cols
        return carry

    lax.fori_loop(0, 4, max_body, 0)
    peak_src = max_cols[...].T[0:8]
    row_n = lax.broadcasted_iota(jnp.int32, (8, N), 0)
    dst_up = pltpu.roll(score, 4, 0)
    peak = jnp.where(peak_src == neg, 0.0, leaky(peak_src + dst_up))
    table = split3(jnp.where(row_n < HEADS, peak, score))
    seg = jnp.zeros((32, N), F32)
    for i in range(ZN):
        near = join3(dot(table, dst_hot[i]))
        edge = leaky(r2[i] + pltpu.roll(near, 4, 0))
        live = (row < HEADS) & (dst_ref[i : i + 1, :] >= 0)
        e = jnp.where(live, jnp.exp(jnp.where(live, edge - near, 0.0)), 0.0)
        expo[i] = e
        seg = seg + dot_nt(split3(e), dst_hot[i])
    seg3 = split3(join3(seg))
    for i in range(ZN):
        live = (row < HEADS) & (dst_ref[i : i + 1, :] >= 0)
        under = jnp.where(live, join3(dot(seg3, dst_hot[i])), 1.0)
        alpha = jnp.where(live, expo[i] / under, 0.0)
        s3[i] = jnp.where(row == HEADS, dst_ref[i : i + 1, :].astype(F32), alpha)
    exchange(s3, r3, n_ss, n_rs, z, in_z)

    stage_own(3)
    stage_own(5)
    stage_near(2)
    stage_own(4)
    stage_near(6)
    stage_far(0)
    stage_far(1)
    stage_far(7)
    stage_near(3)
    stage_pick(0)
    stage_near(5)
    stage_far(2)
    stage_pick(1)
    stage_pick(7)

    arrived(s3, r3, n_ss, n_rs, z, in_z)
    for h in range(HEADS):
        al_send[h, 0:8] = r3[:, h, :]
        al_send[h, 8:16] = r3[:, HEADS, :]
    al_all[0] = al_send[r // 2]
    for d in ORDER[:0:-1]:
        to = hop(r, d, RN)
        send(al_send.at[to // 2], al_all.at[8 - d], o_ss.at[d], o_rs.at[8 - d], in_rel(to))

    stage_near(4)
    stage_far(6)
    stage_pick(2)
    stage_far(3)
    stage_pick(6)
    stage_far(5)
    stage_pick(3)
    stage_far(4)
    stage_pick(5)
    stage_pick(4)

    for d in range(1, 8):
        copy(al_send.at[0], al_all.at[d], o_ss.at[d], o_rs.at[d], in_rel(hop(r, d, RN))).wait_recv()

    def part(zt):
        acc = jnp.zeros((N, CB), F32)
        for j in range(0, RN, 2):
            both = []
            for jj in (j, j + 1):
                alpha = al_all[jj, pl.ds(zt, 1), :]
                target = al_all[jj, pl.ds(zt + 8, 1), :]
                both.append(jnp.where(target == iota_n.astype(F32), alpha, 0.0).astype(BF))
            acc = acc + dot(jnp.concatenate(both, axis=1), picked[zt, j * 128 : j * 128 + 256, :])
        return acc

    half = N // 2

    def ring(way, kind):
        to = hop(z, (1 if way == 0 else -1) * (1, 2, 1, 2)[kind], ZN)
        rows = pl.ds(half * way, half) if kind == 1 else pl.ds(0, N)
        return copy(
            zs.at[way, kind, rows], zr.at[way, kind, rows], z_ss.at[way, kind], z_rs.at[way, kind], in_z(to)
        )

    def ring_send(way, kind):
        c = ring(way, kind)
        c.start()
        sent.append(c)

    for way, sign in ((0, 1), (1, -1)):
        zs[way, 0] = part(hop(z, 3 * sign, ZN)).astype(BF)
        ring_send(way, 0)
    far = part(hop(z, 4, ZN)).astype(BF)
    for way in (0, 1):
        rows = slice(half * way, half * (way + 1))
        zs[way, 1, rows] = far[rows]
        ring_send(way, 1)
    for way, sign in ((0, 1), (1, -1)):
        zs[way, 2] = part(hop(z, sign, ZN)).astype(BF)
        ring_send(way, 2)
    mine = [part(hop(z, 2 * sign, ZN)) for sign in (1, -1)]
    own = part(z)
    for way in (0, 1):
        ring(way, 0).wait_recv()
        ring(way, 1).wait_recv()
        rows = slice(half * way, half * (way + 1))
        other = slice(half * (1 - way), half * (2 - way))
        zs[way, 3, rows] = (mine[way][rows] + zr[way, 0, rows].astype(F32) + zr[way, 1, rows].astype(F32)).astype(BF)
        zs[way, 3, other] = (mine[way][other] + zr[way, 0, other].astype(F32)).astype(BF)
        ring_send(way, 3)
    for way in (0, 1):
        ring(way, 2).wait_recv()
        own = own + zr[way, 2].astype(F32)
    for way in (0, 1):
        ring(way, 3).wait_recv()
        own = own + zr[way, 3].astype(F32)
    out_ref[...] = own.astype(BF)
    for c in sent:
        c.wait_send()


def on_device(node_feats, rel_weight, att_src, att_dst, src_row, dst_row):
    src = src_row.reshape(64, 16).T
    dst = dst_row.reshape(64, 16).T
    vmem = pl.BlockSpec(memory_space=pltpu.VMEM)
    hbm = pl.BlockSpec(memory_space=pltpu.HBM)
    tile8 = pltpu.VMEM((8, 8, 128), F32)
    dma = pltpu.SemaphoreType.DMA
    return pl.pallas_call(
        kernel,
        out_shape=jax.ShapeDtypeStruct((N, CB), BF),
        in_specs=[hbm] * 6,
        out_specs=vmem,
        scratch_shapes=[
            pltpu.VMEM((N, D), BF),
            pltpu.VMEM((D, D), BF),
            pltpu.VMEM((1, D), F32), pltpu.VMEM((1, D), F32),
            pltpu.VMEM((16, 64), jnp.int32), pltpu.VMEM((16, 64), jnp.int32),
            pltpu.VMEM((8, 128), jnp.int32), pltpu.VMEM((8, 128), jnp.int32),
            pltpu.VMEM((64, 128), F32),
            pltpu.VMEM((RN, N, CB), BF),
            pltpu.VMEM((G, RN, N, CB), BF),
            pltpu.VMEM((RN, G, 128, N), BF),
            pltpu.VMEM((ZN, D, CB), BF),
            tile8, tile8,
            pltpu.VMEM((8, 128), F32),
            tile8,
            tile8, tile8, tile8, tile8, tile8, tile8,
            pltpu.VMEM((HEADS, 16, 128), F32),
            pltpu.VMEM((RN, 16, 128), F32),
            pltpu.VMEM((N, 128), F32),
            pltpu.VMEM((ZN, N, 128), BF),
            tile8,
            pltpu.VMEM((2, 4, N, CB), BF),
            pltpu.VMEM((2, 4, N, CB), BF),
            dma((6,)),
            dma((8,)), dma((8,)),
            dma((7, 8)), dma((7, 8)),
            dma((8,)), dma((8,)),
            dma((8,)), dma((8,)),
            dma((8,)), dma((8,)),
            dma((8,)), dma((8,)),
            dma((8,)), dma((8,)),
            dma((8,)), dma((8,)),
            dma((2, 4)), dma((2, 4)),
        ],
        compiler_params=pltpu.CompilerParams(
            collective_id=0, has_side_effects=True, vmem_limit_bytes=62 * 1024 * 1024
        ),
    )(node_feats, rel_weight[0], att_src, att_dst, src, dst)


def solution(mesh):
    placed = (
        P("dom", None),
        P("rel", None, None),
        P("rel", None),
        P("rel", None),
        P("rel", "dom", None, None),
        P("rel", "dom", None, None),
    )
    return jax.shard_map(
        on_device, mesh=mesh, in_specs=placed, out_specs=P("dom", "rel"), check_vma=False
    )
```

```python
import jax
import jax.numpy as jnp
from jax import lax
from jax.experimental import pallas as pl
from jax.experimental.pallas import tpu as pltpu
from jax.sharding import PartitionSpec as P

MESH = pl.DeviceIdType.MESH
HEADS = 4
N = 256
D = 1024
CB = 128
G = 8
ZN = 8
RN = 8
F32 = jnp.float32
BF = jnp.bfloat16
ORDER = (0, 1, 7, 2, 6, 3, 5, 4)
TO_RIGHT = (0, 7, 2, 5)


def split3(v):
    hi = v.astype(BF).astype(F32)
    rest = v - hi
    mid = rest.astype(BF).astype(F32)
    low = rest - mid
    return jnp.concatenate([hi, mid, low, jnp.zeros_like(v)], axis=0).astype(BF)


def join3(v):
    return v[0:8] + v[8:16] + v[16:24]


def leaky(v):
    return jnp.where(v >= 0, v, 0.2 * v)


def dot(a, b):
    return jnp.dot(a, b, preferred_element_type=F32)


def dot_nt(a, b):
    return lax.dot_general(a, b, (((1,), (1,)), ((), ())), preferred_element_type=F32)


def block_transpose(tiles):
    lane_block = lax.broadcasted_iota(jnp.int32, (8, 128), 1) // 16
    for bit in (1, 2, 4):
        low = (lane_block & bit) == 0
        out = list(tiles)
        for i in range(8):
            if i & bit:
                continue
            first, second = tiles[i], tiles[i + bit]
            out[i] = jnp.where(low, first, pltpu.roll(second, 16 * bit, 1))
            out[i + bit] = jnp.where(low, pltpu.roll(first, 128 - 16 * bit, 1), second)
        tiles = out
    return tiles


def kernel(
    feat_ref, w_ref, asrc_hbm, adst_hbm, src_hbm, dst_hbm, out_ref,
    x_buf, w_buf, asrc_ref, adst_ref, src_raw, dst_raw, src_ref, dst_ref, spread, proj, pall, onehot, picked,
    idx_send, idx_recv, idx_rows, idx_all,
    s1, r1, s2, r2, s3, r3, al_send, al_all,
    max_cols, dst_hot, expo,
    zs, zr,
    in_sem, w_sem, y_ss, y_rs, x_ss, x_rs, g_ss, g_rs, h_ss, h_rs, k_ss, k_rs, m_ss, m_rs, n_ss, n_rs, o_ss, o_rs, z_ss, z_rs,
):
    r = lax.axis_index("rel")
    p = lax.axis_index("dom")
    z, g = p // G, p % G
    x, a = g // 2, g % 2
    load_x = pltpu.make_async_copy(feat_ref, x_buf, in_sem.at[0])
    load_w = [
        pltpu.make_async_copy(w_ref.at[:, 256 * i : 256 * (i + 1)], w_buf.at[:, 256 * i : 256 * (i + 1)], w_sem.at[i])
        for i in range(4)
    ]
    load_src = pltpu.make_async_copy(src_hbm, src_raw, in_sem.at[2])
    load_dst = pltpu.make_async_copy(dst_hbm, dst_raw, in_sem.at[3])
    load_as = pltpu.make_async_copy(asrc_hbm, asrc_ref, in_sem.at[4])
    load_ad = pltpu.make_async_copy(adst_hbm, adst_ref, in_sem.at[5])
    for load in (load_x, *load_w, load_src, load_dst, load_as, load_ad):
        load.start()

    def in_group(i):
        return (r, z * G + i)

    def in_z(i):
        return (r, i * G + g)

    def in_rel(i):
        return (i, p)

    def hop(i, amount, size):
        return lax.rem(i + amount + size, size)

    barrier = pltpu.get_barrier_semaphore()
    for d in range(1, 8):
        for dev in (in_group(hop(g, d, G)), in_z(hop(z, d, ZN)), in_rel(hop(r, d, RN))):
            pl.semaphore_signal(barrier, inc=1, device_id=dev, device_id_type=MESH)

    lane_block = lax.broadcasted_iota(jnp.int32, (8, 128), 1) // 16
    load_src.wait()
    spread[...] = jnp.concatenate([src_raw[...].astype(F32)] * 8, axis=0).T
    src_f = jnp.zeros((8, 128), F32)
    for i in range(ZN):
        src_f = jnp.where(lane_block == i, spread[8 * i : 8 * i + 8, :], src_f)
    src_ref[...] = src_f.astype(jnp.int32)
    load_dst.wait()
    spread[...] = jnp.concatenate([dst_raw[...].astype(F32)] * 8, axis=0).T
    dst_f = jnp.zeros((8, 128), F32)
    for i in range(G):
        dst_f = jnp.where(lane_block == i, spread[pl.ds(i, 8, stride=8), :], dst_f)
    dst_ref[...] = dst_f.astype(jnp.int32)
    idx_rows[...] = src_f
    idx_all[0] = src_f

    sent = []

    def copy(src, dst, ss, rs, dev):
        return pltpu.make_async_remote_copy(
            src_ref=src, dst_ref=dst, send_sem=ss, recv_sem=rs, device_id=dev, device_id_type=MESH
        )

    def send(*args):
        c = copy(*args)
        c.start()
        sent.append(c)

    def exchange(sbuf, rbuf, ss, rs, me, member):
        rbuf[me] = sbuf[me]
        for d in ORDER[:0:-1]:
            to = hop(me, d, 8)
            send(sbuf.at[to], rbuf.at[me], ss.at[d], rs.at[8 - d], member(to))

    def arrived(sbuf, rbuf, ss, rs, me, member):
        for d in range(1, 8):
            frm = hop(me, d, 8)
            copy(sbuf.at[frm], rbuf.at[frm], ss.at[d], rs.at[d], member(frm)).wait_recv()

    load_x.wait()
    feats = x_buf[...]
    for i in range(4):
        load_w[i].wait()
        part = dot(feats, w_buf[:, 256 * i : 256 * (i + 1)]).astype(BF)
        proj[2 * i] = part[:, :CB]
        proj[2 * i + 1] = part[:, CB:]

    pl.semaphore_wait(barrier, 21)

    for d in ORDER[:0:-1]:
        send(idx_rows, idx_all.at[8 - d], h_ss.at[d], h_rs.at[8 - d], in_rel(hop(r, d, RN)))
    pall[g, 0] = proj[r]
    def y_send(*ds):
        for d in ds:
            to = hop(r, d, RN)
            send(proj.at[to], pall.at[g, 8 - d], y_ss.at[d], y_rs.at[8 - d], in_rel(to))

    y_send(1, 7, 2, 6)

    x_r, x_l, x_2 = hop(x, 1, 4), hop(x, 3, 4), hop(x, 2, 4)
    g_r, g_l, g_2 = 2 * x_r + a, 2 * x_l + a, 2 * x_2 + a
    partner = 2 * x + 1 - a

    def give(kind, j, owner, to):
        send(pall.at[owner, j], pall.at[owner, j], x_ss.at[kind, j], x_rs.at[kind, j], in_group(to))

    def got(kind, j, owner):
        copy(pall.at[owner, j], pall.at[owner, j], x_ss.at[kind, j], x_rs.at[kind, j], in_group(partner)).wait_recv()

    def stage_own(j):
        if j:
            copy(proj.at[0], pall.at[g, j], y_ss.at[j], y_rs.at[j], in_rel(hop(r, j, RN))).wait_recv()
        give(0, j, g, g_r)
        give(1, j, g, g_l)
        give(3, j, g, partner)

    def stage_near(j):
        got(0, j, g_l)
        if j in TO_RIGHT:
            give(2, j, g_l, g_r)
        give(4, j, g_l, partner)
        got(1, j, g_r)
        if j not in TO_RIGHT:
            give(2, j, g_r, g_l)
        give(5, j, g_r, partner)

    def stage_far(j):
        got(2, j, g_2)
        give(6, j, g_2, partner)

    def stage_pick(j):
        got(3, j, partner)
        got(4, j, 2 * x_l + 1 - a)
        got(5, j, 2 * x_r + 1 - a)
        got(6, j, 2 * x_2 + 1 - a)

        for i in range(G):
            rows = dot(onehot[j, i], pall[i, j]).astype(BF)
            k = j * 128 + i * 16
            picked[:, k : k + 16, :] = rows.reshape(ZN, 16, CB)


    def scores():
        load_as.wait()
        load_ad.wait()
        row8 = lax.broadcasted_iota(jnp.int32, (8, D), 0)
        lane8 = lax.broadcasted_iota(jnp.int32, (8, D), 1)
        att = jnp.where(row8 < HEADS, asrc_ref[...], adst_ref[...])
        att = split3(jnp.where(lane8 // (D // HEADS) == row8 % HEADS, att, 0.0))
        total = jnp.zeros((32, N), F32)
        for c in range(RN):
            total = total + dot_nt(att[:, CB * c : CB * (c + 1)], proj[c])
        score = join3(total)
        score3 = split3(score)

        iota_n = lax.broadcasted_iota(jnp.int32, (N, 128), 0)
        src_i = src_ref[...]
        for i in range(G):
            hot = jnp.where(src_i[i : i + 1] == iota_n, 1.0, 0.0).astype(BF)
            s1[i] = join3(dot(score3, hot))

        exchange(s1, r1, k_ss, k_rs, g, in_group)
        return score, iota_n

    def rows_to_group():
        for d in range(1, 8):
            copy(idx_rows, idx_all.at[d], h_ss.at[d], h_rs.at[d], in_rel(hop(r, d, RN))).wait_recv()
        for i in range(G):
            idx_send[i] = idx_all[:, i, :]
        exchange(idx_send, idx_recv, g_ss, g_rs, g, in_group)

    def scores_along_z():
        arrived(s1, r1, k_ss, k_rs, g, in_group)
        for i, tile in enumerate(block_transpose([r1[i] for i in range(G)])):
            s2[i] = tile
        exchange(s2, r2, m_ss, m_rs, z, in_z)

    def hot_wait():
        arrived(idx_send, idx_recv, g_ss, g_rs, g, in_group)

    def hot(i):
        iota_l = lax.broadcasted_iota(jnp.int32, (128, N), 1).astype(F32)
        cols = idx_recv[i].T
        for j in range(RN):
            onehot[j, i] = jnp.where(cols[:, j : j + 1] == iota_l, 1.0, 0.0).astype(BF)

    def softmax():
        arrived(s2, r2, m_ss, m_rs, z, in_z)
        row = lax.broadcasted_iota(jnp.int32, (8, 128), 0)
        lane = lax.broadcasted_iota(jnp.int32, (64, 128), 1)
        neg = -jnp.inf

        def max_body(t, carry):
            base = pl.multiple_of(t * 64, 64)
            iota_t = lax.broadcasted_iota(jnp.int32, (64, 128), 0) + base
            best = [jnp.full((64, 128), neg, F32) for _ in range(HEADS)]
            for i in range(ZN):
                mask = dst_ref[i : i + 1, :] == iota_t
                dst_hot[i, pl.ds(base, 64), :] = jnp.where(mask, 1.0, 0.0).astype(BF)
                for h in range(HEADS):
                    best[h] = jnp.maximum(best[h], jnp.where(mask, r2[i, h : h + 1, :], neg))
            cols = jnp.zeros((64, 128), F32)
            for h in range(HEADS):
                cols = jnp.where(lane == h, jnp.max(best[h], axis=1, keepdims=True), cols)
            max_cols[pl.ds(base, 64), :] = cols
            return carry

        lax.fori_loop(0, 4, max_body, 0)
        peak_src = max_cols[...].T[0:8]
        row_n = lax.broadcasted_iota(jnp.int32, (8, N), 0)
        dst_up = pltpu.roll(score, 4, 0)
        peak = jnp.where(peak_src == neg, 0.0, leaky(peak_src + dst_up))
        table = split3(jnp.where(row_n < HEADS, peak, score))
        seg = jnp.zeros((32, N), F32)
        for i in range(ZN):
            near = join3(dot(table, dst_hot[i]))
            edge = leaky(r2[i] + pltpu.roll(near, 4, 0))
            live = (row < HEADS) & (dst_ref[i : i + 1, :] >= 0)
            e = jnp.where(live, jnp.exp(jnp.where(live, edge - near, 0.0)), 0.0)
            expo[i] = e
            seg = seg + dot_nt(split3(e), dst_hot[i])
        seg3 = split3(join3(seg))
        for i in range(ZN):
            live = (row < HEADS) & (dst_ref[i : i + 1, :] >= 0)
            under = jnp.where(live, join3(dot(seg3, dst_hot[i])), 1.0)
            alpha = jnp.where(live, expo[i] / under, 0.0)
            s3[i] = jnp.where(row == HEADS, dst_ref[i : i + 1, :].astype(F32), alpha)
        exchange(s3, r3, n_ss, n_rs, z, in_z)

    def coefficients():
        arrived(s3, r3, n_ss, n_rs, z, in_z)
        for h in range(HEADS):
            al_send[h, 0:8] = r3[:, h, :]
            al_send[h, 8:16] = r3[:, HEADS, :]
        al_all[0] = al_send[r // 2]
        for d in ORDER[:0:-1]:
            to = hop(r, d, RN)
            send(al_send.at[to // 2], al_all.at[8 - d], o_ss.at[d], o_rs.at[8 - d], in_rel(to))

    stage_own(0)
    score, iota_n = scores()
    rows_to_group()
    stage_own(1)
    stage_own(7)
    y_send(3,5)
    scores_along_z()
    stage_near(0)
    stage_own(2)
    stage_own(6)
    y_send(4)
    stage_near(1)
    stage_near(7)
    softmax()
    stage_own(3)
    stage_own(5)
    stage_near(2)
    stage_own(4)
    stage_near(6)
    stage_far(0)
    stage_far(1)
    stage_far(7)
    stage_near(3)
    hot_wait()
    for i in range(G):
        hot(i)
    stage_pick(0)
    stage_near(5)
    stage_far(2)
    stage_pick(1)
    stage_pick(7)
    coefficients()
    stage_near(4)
    stage_far(6)
    stage_pick(2)
    stage_far(3)
    stage_pick(6)
    stage_far(5)
    stage_pick(3)
    stage_far(4)
    stage_pick(5)
    stage_pick(4)

    for d in range(1, 8):
        copy(al_send.at[0], al_all.at[d], o_ss.at[d], o_rs.at[d], in_rel(hop(r, d, RN))).wait_recv()

    def part(zt):
        acc = jnp.zeros((N, CB), F32)
        for j in range(0, RN, 2):
            both = []
            for jj in (j, j + 1):
                alpha = al_all[jj, pl.ds(zt, 1), :]
                target = al_all[jj, pl.ds(zt + 8, 1), :]
                both.append(jnp.where(target == iota_n.astype(F32), alpha, 0.0).astype(BF))
            acc = acc + dot(jnp.concatenate(both, axis=1), picked[zt, j * 128 : j * 128 + 256, :])
        return acc

    half = N // 2

    spans = ((0, half), (half, half))

    def ring(way, kind):
        to = hop(z, (1 if way == 0 else -1) * (1, 1, 2, 1, 2, 2)[kind], ZN)
        shared, alone = spans[way], spans[1 - way]
        rows = pl.ds(*(alone, shared, shared, (0, N), alone, shared)[kind])
        slot = (0, 0, 1, 2, 3, 3)[kind]
        return copy(
            zs.at[way, slot, rows], zr.at[way, slot, rows], z_ss.at[way, kind], z_rs.at[way, kind], in_z(to)
        )

    def ring_send(way, kind):
        c = ring(way, kind)
        c.start()
        sent.append(c)

    for way, sign in ((0, 1), (1, -1)):
        zs[way, 0] = part(hop(z, 3 * sign, ZN)).astype(BF)
        ring_send(way, 0)
        ring_send(way, 1)
    far = part(hop(z, 4, ZN)).astype(BF)
    for way in (0, 1):
        rows = slice(half * way, half * (way + 1))
        zs[way, 1, rows] = far[rows]
        ring_send(way, 2)
    for way, sign in ((0, 1), (1, -1)):
        zs[way, 2] = part(hop(z, sign, ZN)).astype(BF)
        ring_send(way, 3)
    mine = [part(hop(z, 2 * sign, ZN)) for sign in (1, -1)]
    for way in (0, 1):
        ring(way, 0).wait_recv()
        rows = slice(half * (1 - way), half * (2 - way))
        zs[way, 3, rows] = (mine[way][rows] + zr[way, 0, rows].astype(F32)).astype(BF)
        ring_send(way, 4)
    own = part(z)
    for way in (0, 1):
        ring(way, 1).wait_recv()
        ring(way, 2).wait_recv()
        rows = slice(half * way, half * (way + 1))
        zs[way, 3, rows] = (mine[way][rows] + zr[way, 0, rows].astype(F32) + zr[way, 1, rows].astype(F32)).astype(BF)
        ring_send(way, 5)
    for way in (0, 1):
        ring(way, 3).wait_recv()
        own = own + zr[way, 2].astype(F32)
    for way in (0, 1):
        ring(way, 4).wait_recv()
    for way in (0, 1):
        ring(way, 5).wait_recv()
        own = own + zr[way, 3].astype(F32)
    out_ref[...] = own.astype(BF)
    for c in sent:
        c.wait_send()


def on_device(node_feats, rel_weight, att_src, att_dst, src_row, dst_row):
    src = src_row.reshape(64, 16).T
    dst = dst_row.reshape(64, 16).T
    vmem = pl.BlockSpec(memory_space=pltpu.VMEM)
    hbm = pl.BlockSpec(memory_space=pltpu.HBM)
    tile8 = pltpu.VMEM((8, 8, 128), F32)
    dma = pltpu.SemaphoreType.DMA
    return pl.pallas_call(
        kernel,
        out_shape=pltpu.VMEM((N, CB), BF),
        in_specs=[hbm] * 6,
        out_specs=vmem,
        scratch_shapes=[
            pltpu.VMEM((N, D), BF),
            pltpu.VMEM((D, D), BF),
            pltpu.VMEM((1, D), F32), pltpu.VMEM((1, D), F32),
            pltpu.VMEM((16, 64), jnp.int32), pltpu.VMEM((16, 64), jnp.int32),
            pltpu.VMEM((8, 128), jnp.int32), pltpu.VMEM((8, 128), jnp.int32),
            pltpu.VMEM((64, 128), F32),
            pltpu.VMEM((RN, N, CB), BF),
            pltpu.VMEM((G, RN, N, CB), BF),
            pltpu.VMEM((RN, G, 128, N), BF),
            pltpu.VMEM((ZN, D, CB), BF),
            tile8, tile8,
            pltpu.VMEM((8, 128), F32),
            tile8,
            tile8, tile8, tile8, tile8, tile8, tile8,
            pltpu.VMEM((HEADS, 16, 128), F32),
            pltpu.VMEM((RN, 16, 128), F32),
            pltpu.VMEM((N, 128), F32),
            pltpu.VMEM((ZN, N, 128), BF),
            tile8,
            pltpu.VMEM((2, 4, N, CB), BF),
            pltpu.VMEM((2, 4, N, CB), BF),
            dma((6,)), dma((4,)),
            dma((8,)), dma((8,)),
            dma((7, 8)), dma((7, 8)),
            dma((8,)), dma((8,)),
            dma((8,)), dma((8,)),
            dma((8,)), dma((8,)),
            dma((8,)), dma((8,)),
            dma((8,)), dma((8,)),
            dma((8,)), dma((8,)),
            dma((2, 6)), dma((2, 6)),
        ],
        compiler_params=pltpu.CompilerParams(
            collective_id=0, has_side_effects=True, vmem_limit_bytes=62 * 1024 * 1024
        ),
    )(node_feats, rel_weight[0], att_src, att_dst, src, dst)


def solution(mesh):
    placed = (
        P("dom", None),
        P("rel", None, None),
        P("rel", None),
        P("rel", None),
        P("rel", "dom", None, None),
        P("rel", "dom", None, None),
    )
    return jax.shard_map(
        on_device, mesh=mesh, in_specs=placed, out_specs=P("dom", "rel"), check_vma=False
    )
```

```python
import jax
import jax.numpy as jnp
from jax import lax
from jax.experimental import pallas as pl
from jax.experimental.pallas import tpu as pltpu
from jax.sharding import PartitionSpec as P

MESH = pl.DeviceIdType.MESH
HEADS = 4
N = 256
D = 1024
CB = 128
G = 8
ZN = 8
RN = 8
F32 = jnp.float32
BF = jnp.bfloat16
ORDER = (0, 1, 7, 2, 6, 3, 5, 4)
TO_RIGHT = (0, 7, 2, 5)


def split3(v):
    hi = v.astype(BF).astype(F32)
    rest = v - hi
    mid = rest.astype(BF).astype(F32)
    low = rest - mid
    return jnp.concatenate([hi, mid, low, jnp.zeros_like(v)], axis=0).astype(BF)


def join3(v):
    return v[0:8] + v[8:16] + v[16:24]


def leaky(v):
    return jnp.where(v >= 0, v, 0.2 * v)


def dot(a, b):
    return jnp.dot(a, b, preferred_element_type=F32)


def dot_nt(a, b):
    return lax.dot_general(a, b, (((1,), (1,)), ((), ())), preferred_element_type=F32)


def block_transpose(tiles):
    lane_block = lax.broadcasted_iota(jnp.int32, (8, 128), 1) // 16
    for bit in (1, 2, 4):
        low = (lane_block & bit) == 0
        out = list(tiles)
        for i in range(8):
            if i & bit:
                continue
            first, second = tiles[i], tiles[i + bit]
            out[i] = jnp.where(low, first, pltpu.roll(second, 16 * bit, 1))
            out[i + bit] = jnp.where(low, pltpu.roll(first, 128 - 16 * bit, 1), second)
        tiles = out
    return tiles


def kernel(
    feat_ref, w_ref, asrc_hbm, adst_hbm, src_hbm, dst_hbm, out_ref,
    x_buf, w_buf, asrc_ref, adst_ref, src_raw, dst_raw, src_ref, dst_ref, spread, proj, pall, onehot, picked,
    idx_send, idx_recv, idx_rows, idx_all,
    s1, r1, s2, r2, s3, r3, al_send, al_all,
    max_cols, dst_hot, expo,
    zs, zr,
    in_sem, w_sem, y_ss, y_rs, x_ss, x_rs, g_ss, g_rs, h_ss, h_rs, k_ss, k_rs, m_ss, m_rs, n_ss, n_rs, o_ss, o_rs, z_ss, z_rs,
):
    r = lax.axis_index("rel")
    p = lax.axis_index("dom")
    z, g = p // G, p % G
    x, a = g // 2, g % 2
    load_x = pltpu.make_async_copy(feat_ref, x_buf, in_sem.at[0])
    load_w = [
        pltpu.make_async_copy(w_ref.at[:, 256 * i : 256 * (i + 1)], w_buf.at[:, 256 * i : 256 * (i + 1)], w_sem.at[i])
        for i in range(4)
    ]
    load_src = pltpu.make_async_copy(src_hbm, src_raw, in_sem.at[2])
    load_dst = pltpu.make_async_copy(dst_hbm, dst_raw, in_sem.at[3])
    load_as = pltpu.make_async_copy(asrc_hbm, asrc_ref, in_sem.at[4])
    load_ad = pltpu.make_async_copy(adst_hbm, adst_ref, in_sem.at[5])
    for load in (load_x, *load_w, load_src, load_dst, load_as, load_ad):
        load.start()

    def in_group(i):
        return (r, z * G + i)

    def in_z(i):
        return (r, i * G + g)

    def in_rel(i):
        return (i, p)

    def hop(i, amount, size):
        return lax.rem(i + amount + size, size)

    barrier = pltpu.get_barrier_semaphore()
    for d in range(1, 8):
        for dev in (in_group(hop(g, d, G)), in_z(hop(z, d, ZN)), in_rel(hop(r, d, RN))):
            pl.semaphore_signal(barrier, inc=1, device_id=dev, device_id_type=MESH)

    lane_block = lax.broadcasted_iota(jnp.int32, (8, 128), 1) // 16
    load_src.wait()
    spread[...] = jnp.concatenate([src_raw[...].astype(F32)] * 8, axis=0).T
    src_f = jnp.zeros((8, 128), F32)
    for i in range(ZN):
        src_f = jnp.where(lane_block == i, spread[8 * i : 8 * i + 8, :], src_f)
    src_ref[...] = src_f.astype(jnp.int32)
    load_dst.wait()
    spread[...] = jnp.concatenate([dst_raw[...].astype(F32)] * 8, axis=0).T
    dst_f = jnp.zeros((8, 128), F32)
    for i in range(G):
        dst_f = jnp.where(lane_block == i, spread[pl.ds(i, 8, stride=8), :], dst_f)
    dst_ref[...] = dst_f.astype(jnp.int32)
    idx_rows[...] = src_f
    idx_all[0] = src_f

    sent = []

    def copy(src, dst, ss, rs, dev):
        return pltpu.make_async_remote_copy(
            src_ref=src, dst_ref=dst, send_sem=ss, recv_sem=rs, device_id=dev, device_id_type=MESH
        )

    def send(*args):
        c = copy(*args)
        c.start()
        sent.append(c)

    def exchange(sbuf, rbuf, ss, rs, me, member):
        rbuf[me] = sbuf[me]
        for d in ORDER[:0:-1]:
            to = hop(me, d, 8)
            send(sbuf.at[to], rbuf.at[me], ss.at[d], rs.at[8 - d], member(to))

    def arrived(sbuf, rbuf, ss, rs, me, member):
        for d in range(1, 8):
            frm = hop(me, d, 8)
            copy(sbuf.at[frm], rbuf.at[frm], ss.at[d], rs.at[d], member(frm)).wait_recv()

    load_x.wait()
    feats = x_buf[...]
    for i in range(4):
        load_w[i].wait()
        part = dot(feats, w_buf[:, 256 * i : 256 * (i + 1)]).astype(BF)
        proj[2 * i] = part[:, :CB]
        proj[2 * i + 1] = part[:, CB:]

    pl.semaphore_wait(barrier, 21)

    for d in ORDER[:0:-1]:
        send(idx_rows, idx_all.at[8 - d], h_ss.at[d], h_rs.at[8 - d], in_rel(hop(r, d, RN)))
    pall[g, 0] = proj[r]
    def y_send(*ds):
        for d in ds:
            to = hop(r, d, RN)
            send(proj.at[to], pall.at[g, 8 - d], y_ss.at[d], y_rs.at[8 - d], in_rel(to))

    y_send(1, 7, 2, 6)

    x_r, x_l, x_2 = hop(x, 1, 4), hop(x, 3, 4), hop(x, 2, 4)
    g_r, g_l, g_2 = 2 * x_r + a, 2 * x_l + a, 2 * x_2 + a
    partner = 2 * x + 1 - a

    def give(kind, j, owner, to):
        send(pall.at[owner, j], pall.at[owner, j], x_ss.at[kind, j], x_rs.at[kind, j], in_group(to))

    def got(kind, j, owner):
        copy(pall.at[owner, j], pall.at[owner, j], x_ss.at[kind, j], x_rs.at[kind, j], in_group(partner)).wait_recv()

    def stage_own(j):
        if j:
            copy(proj.at[0], pall.at[g, j], y_ss.at[j], y_rs.at[j], in_rel(hop(r, j, RN))).wait_recv()
        give(0, j, g, g_r)
        give(1, j, g, g_l)
        give(3, j, g, partner)

    def stage_near(j):
        if j in TO_RIGHT:
            got(0, j, g_l)
            give(2, j, g_l, g_r)
            got(1, j, g_r)
        else:
            got(1, j, g_r)
            give(2, j, g_r, g_l)
            got(0, j, g_l)
        give(4, j, g_l, partner)
        give(5, j, g_r, partner)

    def stage_far(j):
        got(2, j, g_2)
        give(6, j, g_2, partner)

    def stage_pick(j):
        got(3, j, partner)
        got(4, j, 2 * x_l + 1 - a)
        got(5, j, 2 * x_r + 1 - a)
        got(6, j, 2 * x_2 + 1 - a)

        for i in range(G):
            rows = dot(onehot[j, i], pall[i, j]).astype(BF)
            k = j * 128 + i * 16
            picked[:, k : k + 16, :] = rows.reshape(ZN, 16, CB)


    def scores():
        load_as.wait()
        load_ad.wait()
        row8 = lax.broadcasted_iota(jnp.int32, (8, D), 0)
        lane8 = lax.broadcasted_iota(jnp.int32, (8, D), 1)
        att = jnp.where(row8 < HEADS, asrc_ref[...], adst_ref[...])
        att = split3(jnp.where(lane8 // (D // HEADS) == row8 % HEADS, att, 0.0))
        total = jnp.zeros((32, N), F32)
        for c in range(RN):
            total = total + dot_nt(att[:, CB * c : CB * (c + 1)], proj[c])
        score = join3(total)
        score3 = split3(score)

        iota_n = lax.broadcasted_iota(jnp.int32, (N, 128), 0)
        src_i = src_ref[...]
        for i in range(G):
            hot = jnp.where(src_i[i : i + 1] == iota_n, 1.0, 0.0).astype(BF)
            s1[i] = join3(dot(score3, hot))

        exchange(s1, r1, k_ss, k_rs, g, in_group)
        return score, iota_n

    def rows_to_group():
        for d in range(1, 8):
            copy(idx_rows, idx_all.at[d], h_ss.at[d], h_rs.at[d], in_rel(hop(r, d, RN))).wait_recv()
        for i in range(G):
            idx_send[i] = idx_all[:, i, :]
        exchange(idx_send, idx_recv, g_ss, g_rs, g, in_group)

    def scores_along_z():
        arrived(s1, r1, k_ss, k_rs, g, in_group)
        for i, tile in enumerate(block_transpose([r1[i] for i in range(G)])):
            s2[i] = tile
        exchange(s2, r2, m_ss, m_rs, z, in_z)

    def hot_wait():
        arrived(idx_send, idx_recv, g_ss, g_rs, g, in_group)

    def hot(i):
        iota_l = lax.broadcasted_iota(jnp.int32, (128, N), 1).astype(F32)
        cols = idx_recv[i].T
        for j in range(RN):
            onehot[j, i] = jnp.where(cols[:, j : j + 1] == iota_l, 1.0, 0.0).astype(BF)

    def softmax():
        arrived(s2, r2, m_ss, m_rs, z, in_z)
        lane = lax.broadcasted_iota(jnp.int32, (64, 128), 1)
        neg = -jnp.inf

        def max_body(t, carry):
            base = pl.multiple_of(t * 64, 64)
            iota_t = lax.broadcasted_iota(jnp.int32, (64, 128), 0) + base
            best = [jnp.full((64, 128), neg, F32) for _ in range(HEADS)]
            for i in range(ZN):
                mask = dst_ref[i : i + 1, :] == iota_t
                dst_hot[i, pl.ds(base, 64), :] = jnp.where(mask, 1.0, 0.0).astype(BF)
                for h in range(HEADS):
                    best[h] = jnp.maximum(best[h], jnp.where(mask, r2[i, h : h + 1, :], neg))
            cols = jnp.zeros((64, 128), F32)
            for h in range(HEADS):
                cols = jnp.where(lane == h, jnp.max(best[h], axis=1, keepdims=True), cols)
            max_cols[pl.ds(base, 64), :] = cols
            return carry

        lax.fori_loop(0, 4, max_body, 0)

    def softmax_rest():
        row = lax.broadcasted_iota(jnp.int32, (8, 128), 0)
        neg = -jnp.inf
        peak_src = max_cols[...].T[0:8]
        row_n = lax.broadcasted_iota(jnp.int32, (8, N), 0)
        dst_up = pltpu.roll(score, 4, 0)
        peak = jnp.where(peak_src == neg, 0.0, leaky(peak_src + dst_up))
        table = split3(jnp.where(row_n < HEADS, peak, score))
        seg = jnp.zeros((32, N), F32)
        for i in range(ZN):
            near = join3(dot(table, dst_hot[i]))
            edge = leaky(r2[i] + pltpu.roll(near, 4, 0))
            live = (row < HEADS) & (dst_ref[i : i + 1, :] >= 0)
            e = jnp.where(live, jnp.exp(jnp.where(live, edge - near, 0.0)), 0.0)
            expo[i] = e
            seg = seg + dot_nt(split3(e), dst_hot[i])
        seg3 = split3(join3(seg))
        for i in range(ZN):
            live = (row < HEADS) & (dst_ref[i : i + 1, :] >= 0)
            under = jnp.where(live, join3(dot(seg3, dst_hot[i])), 1.0)
            alpha = jnp.where(live, expo[i] / under, 0.0)
            s3[i] = jnp.where(row == HEADS, dst_ref[i : i + 1, :].astype(F32), alpha)
        exchange(s3, r3, n_ss, n_rs, z, in_z)

    def coefficients():
        arrived(s3, r3, n_ss, n_rs, z, in_z)
        for h in range(HEADS):
            al_send[h, 0:8] = r3[:, h, :]
            al_send[h, 8:16] = r3[:, HEADS, :]
        al_all[0] = al_send[r // 2]
        for d in ORDER[:0:-1]:
            to = hop(r, d, RN)
            send(al_send.at[to // 2], al_all.at[8 - d], o_ss.at[d], o_rs.at[8 - d], in_rel(to))

    stage_own(0)
    score, iota_n = scores()
    rows_to_group()
    stage_own(1)
    y_send(3)
    stage_own(7)
    y_send(5)
    scores_along_z()
    stage_near(0)
    stage_own(2)
    stage_own(6)
    y_send(4)
    stage_near(1)
    softmax()
    stage_near(7)
    softmax_rest()
    stage_own(3)
    stage_own(5)
    stage_near(2)
    stage_own(4)
    stage_near(6)
    stage_far(0)
    stage_far(1)
    stage_far(7)
    stage_near(3)
    hot_wait()
    for i in range(G):
        hot(i)
    stage_pick(0)
    stage_near(5)
    stage_far(2)
    stage_pick(1)
    coefficients()
    stage_pick(7)
    stage_near(4)
    stage_far(6)
    stage_pick(2)
    stage_far(3)
    stage_pick(6)
    stage_far(5)
    stage_pick(3)
    stage_far(4)
    stage_pick(5)
    stage_pick(4)

    for d in range(1, 8):
        copy(al_send.at[0], al_all.at[d], o_ss.at[d], o_rs.at[d], in_rel(hop(r, d, RN))).wait_recv()

    def part(zt):
        acc = jnp.zeros((N, CB), F32)
        for j in range(0, RN, 2):
            both = []
            for jj in (j, j + 1):
                alpha = al_all[jj, pl.ds(zt, 1), :]
                target = al_all[jj, pl.ds(zt + 8, 1), :]
                both.append(jnp.where(target == iota_n.astype(F32), alpha, 0.0).astype(BF))
            acc = acc + dot(jnp.concatenate(both, axis=1), picked[zt, j * 128 : j * 128 + 256, :])
        return acc

    half = N // 2

    spans = ((0, half), (half, half))

    def ring(way, kind):
        to = hop(z, (1 if way == 0 else -1) * (1, 1, 2, 1, 2, 2)[kind], ZN)
        shared, alone = spans[way], spans[1 - way]
        rows = pl.ds(*(alone, shared, shared, (0, N), alone, shared)[kind])
        slot = (0, 0, 1, 2, 3, 3)[kind]
        return copy(
            zs.at[way, slot, rows], zr.at[way, slot, rows], z_ss.at[way, kind], z_rs.at[way, kind], in_z(to)
        )

    def ring_send(way, kind):
        c = ring(way, kind)
        c.start()
        sent.append(c)

    before = tuple(sent)
    sent.clear()
    for way, sign in ((0, 1), (1, -1)):
        zs[way, 0] = part(hop(z, 3 * sign, ZN)).astype(BF)
        ring_send(way, 0)
        ring_send(way, 1)
    far = part(hop(z, 4, ZN)).astype(BF)
    for way in (0, 1):
        rows = slice(half * way, half * (way + 1))
        zs[way, 1, rows] = far[rows]
        ring_send(way, 2)
    for way, sign in ((0, 1), (1, -1)):
        zs[way, 2] = part(hop(z, sign, ZN)).astype(BF)
        ring_send(way, 3)
    mine = [part(hop(z, 2 * sign, ZN)) for sign in (1, -1)]
    for c in before:
        c.wait_send()
    for way in (0, 1):
        ring(way, 0).wait_recv()
        rows = slice(half * (1 - way), half * (2 - way))
        zs[way, 3, rows] = (mine[way][rows] + zr[way, 0, rows].astype(F32)).astype(BF)
        ring_send(way, 4)
    own = part(z)
    for way in (0, 1):
        ring(way, 1).wait_recv()
        ring(way, 2).wait_recv()
        rows = slice(half * way, half * (way + 1))
        zs[way, 3, rows] = (mine[way][rows] + zr[way, 0, rows].astype(F32) + zr[way, 1, rows].astype(F32)).astype(BF)
        ring_send(way, 5)
    for way in (0, 1):
        ring(way, 3).wait_recv()
        own = own + zr[way, 2].astype(F32)
    for way in (0, 1):
        ring(way, 4).wait_recv()
    for way in (0, 1):
        ring(way, 5).wait_recv()
        own = own + zr[way, 3].astype(F32)
    out_ref[...] = own.astype(BF)
    for c in sent:
        c.wait_send()


def on_device(node_feats, rel_weight, att_src, att_dst, src_row, dst_row):
    src = src_row.reshape(64, 16).T
    dst = dst_row.reshape(64, 16).T
    vmem = pl.BlockSpec(memory_space=pltpu.VMEM)
    hbm = pl.BlockSpec(memory_space=pltpu.HBM)
    tile8 = pltpu.VMEM((8, 8, 128), F32)
    dma = pltpu.SemaphoreType.DMA
    return pl.pallas_call(
        kernel,
        out_shape=pltpu.VMEM((N, CB), BF),
        in_specs=[hbm] * 6,
        out_specs=vmem,
        scratch_shapes=[
            pltpu.VMEM((N, D), BF),
            pltpu.VMEM((D, D), BF),
            pltpu.VMEM((1, D), F32), pltpu.VMEM((1, D), F32),
            pltpu.VMEM((16, 64), jnp.int32), pltpu.VMEM((16, 64), jnp.int32),
            pltpu.VMEM((8, 128), jnp.int32), pltpu.VMEM((8, 128), jnp.int32),
            pltpu.VMEM((64, 128), F32),
            pltpu.VMEM((RN, N, CB), BF),
            pltpu.VMEM((G, RN, N, CB), BF),
            pltpu.VMEM((RN, G, 128, N), BF),
            pltpu.VMEM((ZN, D, CB), BF),
            tile8, tile8,
            pltpu.VMEM((8, 128), F32),
            tile8,
            tile8, tile8, tile8, tile8, tile8, tile8,
            pltpu.VMEM((HEADS, 16, 128), F32),
            pltpu.VMEM((RN, 16, 128), F32),
            pltpu.VMEM((N, 128), F32),
            pltpu.VMEM((ZN, N, 128), BF),
            tile8,
            pltpu.VMEM((2, 4, N, CB), BF),
            pltpu.VMEM((2, 4, N, CB), BF),
            dma((6,)), dma((4,)),
            dma((8,)), dma((8,)),
            dma((7, 8)), dma((7, 8)),
            dma((8,)), dma((8,)),
            dma((8,)), dma((8,)),
            dma((8,)), dma((8,)),
            dma((8,)), dma((8,)),
            dma((8,)), dma((8,)),
            dma((8,)), dma((8,)),
            dma((2, 6)), dma((2, 6)),
        ],
        compiler_params=pltpu.CompilerParams(
            collective_id=0, has_side_effects=True, vmem_limit_bytes=62 * 1024 * 1024
        ),
    )(node_feats, rel_weight[0], att_src, att_dst, src, dst)


def solution(mesh):
    placed = (
        P("dom", None),
        P("rel", None, None),
        P("rel", None),
        P("rel", None),
        P("rel", "dom", None, None),
        P("rel", "dom", None, None),
    )
    return jax.shard_map(
        on_device, mesh=mesh, in_specs=placed, out_specs=P("dom", "rel"), check_vma=False
    )
```

```python
import jax
import jax.numpy as jnp
from jax import lax
from jax.experimental import pallas as pl
from jax.experimental.pallas import tpu as pltpu
from jax.sharding import PartitionSpec as P

MESH = pl.DeviceIdType.MESH
HEADS = 4
N = 256
D = 1024
CB = 128
G = 8
ZN = 8
RN = 8
F32 = jnp.float32
BF = jnp.bfloat16
ORDER = (0, 1, 7, 2, 6, 3, 5, 4)
TO_RIGHT = (0, 7, 2, 5)


def split3(v):
    hi = v.astype(BF).astype(F32)
    rest = v - hi
    mid = rest.astype(BF).astype(F32)
    low = rest - mid
    return jnp.concatenate([hi, mid, low, jnp.zeros_like(v)], axis=0).astype(BF)


def join3(v):
    return v[0:8] + v[8:16] + v[16:24]


def leaky(v):
    return jnp.where(v >= 0, v, 0.2 * v)


def dot(a, b):
    return jnp.dot(a, b, preferred_element_type=F32)


def dot_nt(a, b):
    return lax.dot_general(a, b, (((1,), (1,)), ((), ())), preferred_element_type=F32)


def block_transpose(tiles):
    lane_block = lax.broadcasted_iota(jnp.int32, (8, 128), 1) // 16
    for bit in (1, 2, 4):
        low = (lane_block & bit) == 0
        out = list(tiles)
        for i in range(8):
            if i & bit:
                continue
            first, second = tiles[i], tiles[i + bit]
            out[i] = jnp.where(low, first, pltpu.roll(second, 16 * bit, 1))
            out[i + bit] = jnp.where(low, pltpu.roll(first, 128 - 16 * bit, 1), second)
        tiles = out
    return tiles


def kernel(
    feat_ref, w_ref, asrc_hbm, adst_hbm, src_hbm, dst_hbm, out_ref,
    x_buf, w_buf, asrc_ref, adst_ref, src_raw, dst_raw, src_ref, dst_ref, spread, proj, pall, onehot, picked,
    idx_send, idx_recv, idx_rows, idx_all,
    s1, r1, s2, r2, s3, r3, al_send, al_all,
    max_cols, dst_hot, expo,
    zs, zr,
    in_sem, w_sem, y_ss, y_rs, x_ss, x_rs, g_ss, g_rs, h_ss, h_rs, k_ss, k_rs, m_ss, m_rs, n_ss, n_rs, o_ss, o_rs, z_ss, z_rs,
):
    r = lax.axis_index("rel")
    p = lax.axis_index("dom")
    z, g = p // G, p % G
    x, a = g // 2, g % 2
    load_x = pltpu.make_async_copy(feat_ref, x_buf, in_sem.at[0])
    load_w = [
        pltpu.make_async_copy(w_ref.at[:, 256 * i : 256 * (i + 1)], w_buf.at[:, 256 * i : 256 * (i + 1)], w_sem.at[i])
        for i in range(4)
    ]
    load_src = pltpu.make_async_copy(src_hbm, src_raw, in_sem.at[2])
    load_dst = pltpu.make_async_copy(dst_hbm, dst_raw, in_sem.at[3])
    load_as = pltpu.make_async_copy(asrc_hbm, asrc_ref, in_sem.at[4])
    load_ad = pltpu.make_async_copy(adst_hbm, adst_ref, in_sem.at[5])
    for load in (load_x, *load_w, load_src, load_dst, load_as, load_ad):
        load.start()

    def in_group(i):
        return (r, z * G + i)

    def in_z(i):
        return (r, i * G + g)

    def in_rel(i):
        return (i, p)

    def hop(i, amount, size):
        return lax.rem(i + amount + size, size)

    barrier = pltpu.get_barrier_semaphore()
    for d in range(1, 8):
        for dev in (in_group(hop(g, d, G)), in_z(hop(z, d, ZN)), in_rel(hop(r, d, RN))):
            pl.semaphore_signal(barrier, inc=1, device_id=dev, device_id_type=MESH)

    lane_block = lax.broadcasted_iota(jnp.int32, (8, 128), 1) // 16
    load_src.wait()
    spread[...] = jnp.concatenate([src_raw[...].astype(F32)] * 8, axis=0).T
    src_f = jnp.zeros((8, 128), F32)
    for i in range(ZN):
        src_f = jnp.where(lane_block == i, spread[8 * i : 8 * i + 8, :], src_f)
    src_ref[...] = src_f.astype(jnp.int32)
    load_dst.wait()
    spread[...] = jnp.concatenate([dst_raw[...].astype(F32)] * 8, axis=0).T
    dst_f = jnp.zeros((8, 128), F32)
    for i in range(G):
        dst_f = jnp.where(lane_block == i, spread[pl.ds(i, 8, stride=8), :], dst_f)
    dst_ref[...] = dst_f.astype(jnp.int32)
    idx_rows[...] = src_f
    idx_all[0] = src_f

    sent = []

    def copy(src, dst, ss, rs, dev):
        return pltpu.make_async_remote_copy(
            src_ref=src, dst_ref=dst, send_sem=ss, recv_sem=rs, device_id=dev, device_id_type=MESH
        )

    def send(*args):
        c = copy(*args)
        c.start()
        sent.append(c)

    def exchange(sbuf, rbuf, ss, rs, me, member):
        rbuf[me] = sbuf[me]
        for d in ORDER[:0:-1]:
            to = hop(me, d, 8)
            send(sbuf.at[to], rbuf.at[me], ss.at[d], rs.at[8 - d], member(to))

    def arrived(sbuf, rbuf, ss, rs, me, member):
        for d in range(1, 8):
            frm = hop(me, d, 8)
            copy(sbuf.at[frm], rbuf.at[frm], ss.at[d], rs.at[d], member(frm)).wait_recv()

    load_x.wait()
    feats = x_buf[...]
    for i in range(4):
        load_w[i].wait()
        part = dot(feats, w_buf[:, 256 * i : 256 * (i + 1)]).astype(BF)
        proj[2 * i] = part[:, :CB]
        proj[2 * i + 1] = part[:, CB:]

    pl.semaphore_wait(barrier, 21)

    for d in ORDER[:0:-1]:
        send(idx_rows, idx_all.at[8 - d], h_ss.at[d], h_rs.at[8 - d], in_rel(hop(r, d, RN)))
    pall[g, 0] = proj[r]
    def y_send(*ds):
        for d in ds:
            to = hop(r, d, RN)
            send(proj.at[to], pall.at[g, 8 - d], y_ss.at[d], y_rs.at[8 - d], in_rel(to))

    y_send(1, 7, 2, 6)

    x_r, x_l, x_2 = hop(x, 1, 4), hop(x, 3, 4), hop(x, 2, 4)
    g_r, g_l, g_2 = 2 * x_r + a, 2 * x_l + a, 2 * x_2 + a
    partner = 2 * x + 1 - a

    def give(kind, j, owner, to):
        send(pall.at[owner, j], pall.at[owner, j], x_ss.at[kind, j], x_rs.at[kind, j], in_group(to))

    def got(kind, j, owner):
        copy(pall.at[owner, j], pall.at[owner, j], x_ss.at[kind, j], x_rs.at[kind, j], in_group(partner)).wait_recv()

    def stage_own(j):
        if j:
            copy(proj.at[0], pall.at[g, j], y_ss.at[j], y_rs.at[j], in_rel(hop(r, j, RN))).wait_recv()
        give(0, j, g, g_r)
        give(1, j, g, g_l)

    def stage_near(j):
        if j in TO_RIGHT:
            got(0, j, g_l)
            give(2, j, g_l, g_r)
            got(1, j, g_r)
        else:
            got(1, j, g_r)
            give(2, j, g_r, g_l)
            got(0, j, g_l)
        give(3, j, g, partner)
        give(4, j, g_l, partner)
        give(5, j, g_r, partner)

    def stage_far(j):
        got(2, j, g_2)
        give(6, j, g_2, partner)

    def stage_pick(j):
        got(3, j, partner)
        got(4, j, 2 * x_l + 1 - a)
        got(5, j, 2 * x_r + 1 - a)
        got(6, j, 2 * x_2 + 1 - a)

        for i in range(G):
            rows = dot(onehot[j, i], pall[i, j]).astype(BF)
            k = j * 128 + i * 16
            picked[:, k : k + 16, :] = rows.reshape(ZN, 16, CB)


    def scores():
        load_as.wait()
        load_ad.wait()
        row8 = lax.broadcasted_iota(jnp.int32, (8, D), 0)
        lane8 = lax.broadcasted_iota(jnp.int32, (8, D), 1)
        att = jnp.where(row8 < HEADS, asrc_ref[...], adst_ref[...])
        att = split3(jnp.where(lane8 // (D // HEADS) == row8 % HEADS, att, 0.0))
        total = jnp.zeros((32, N), F32)
        for c in range(RN):
            total = total + dot_nt(att[:, CB * c : CB * (c + 1)], proj[c])
        score = join3(total)
        score3 = split3(score)

        iota_n = lax.broadcasted_iota(jnp.int32, (N, 128), 0)
        src_i = src_ref[...]
        for i in range(G):
            hot = jnp.where(src_i[i : i + 1] == iota_n, 1.0, 0.0).astype(BF)
            s1[i] = join3(dot(score3, hot))

        exchange(s1, r1, k_ss, k_rs, g, in_group)
        return score, iota_n

    def rows_to_group():
        for d in range(1, 8):
            copy(idx_rows, idx_all.at[d], h_ss.at[d], h_rs.at[d], in_rel(hop(r, d, RN))).wait_recv()
        for i in range(G):
            idx_send[i] = idx_all[:, i, :]
        exchange(idx_send, idx_recv, g_ss, g_rs, g, in_group)

    def scores_along_z():
        arrived(s1, r1, k_ss, k_rs, g, in_group)
        for i, tile in enumerate(block_transpose([r1[i] for i in range(G)])):
            s2[i] = tile
        exchange(s2, r2, m_ss, m_rs, z, in_z)

    def hot_wait():
        arrived(idx_send, idx_recv, g_ss, g_rs, g, in_group)

    def hot(i):
        iota_l = lax.broadcasted_iota(jnp.int32, (128, N), 1).astype(F32)
        cols = idx_recv[i].T
        for j in range(RN):
            onehot[j, i] = jnp.where(cols[:, j : j + 1] == iota_l, 1.0, 0.0).astype(BF)

    def softmax():
        arrived(s2, r2, m_ss, m_rs, z, in_z)
        lane = lax.broadcasted_iota(jnp.int32, (64, 128), 1)
        neg = -jnp.inf

        def max_body(t, carry):
            base = pl.multiple_of(t * 64, 64)
            iota_t = lax.broadcasted_iota(jnp.int32, (64, 128), 0) + base
            best = [jnp.full((64, 128), neg, F32) for _ in range(HEADS)]
            for i in range(ZN):
                mask = dst_ref[i : i + 1, :] == iota_t
                dst_hot[i, pl.ds(base, 64), :] = jnp.where(mask, 1.0, 0.0).astype(BF)
                for h in range(HEADS):
                    best[h] = jnp.maximum(best[h], jnp.where(mask, r2[i, h : h + 1, :], neg))
            cols = jnp.zeros((64, 128), F32)
            for h in range(HEADS):
                cols = jnp.where(lane == h, jnp.max(best[h], axis=1, keepdims=True), cols)
            max_cols[pl.ds(base, 64), :] = cols
            return carry

        lax.fori_loop(0, 4, max_body, 0)

    def softmax_rest():
        row = lax.broadcasted_iota(jnp.int32, (8, 128), 0)
        neg = -jnp.inf
        peak_src = max_cols[...].T[0:8]
        row_n = lax.broadcasted_iota(jnp.int32, (8, N), 0)
        dst_up = pltpu.roll(score, 4, 0)
        peak = jnp.where(peak_src == neg, 0.0, leaky(peak_src + dst_up))
        table = split3(jnp.where(row_n < HEADS, peak, score))
        seg = jnp.zeros((32, N), F32)
        for i in range(ZN):
            near = join3(dot(table, dst_hot[i]))
            edge = leaky(r2[i] + pltpu.roll(near, 4, 0))
            live = (row < HEADS) & (dst_ref[i : i + 1, :] >= 0)
            e = jnp.where(live, jnp.exp(jnp.where(live, edge - near, 0.0)), 0.0)
            expo[i] = e
            seg = seg + dot_nt(split3(e), dst_hot[i])
        seg3 = split3(join3(seg))
        for i in range(ZN):
            live = (row < HEADS) & (dst_ref[i : i + 1, :] >= 0)
            under = jnp.where(live, join3(dot(seg3, dst_hot[i])), 1.0)
            alpha = jnp.where(live, expo[i] / under, 0.0)
            s3[i] = jnp.where(row == HEADS, dst_ref[i : i + 1, :].astype(F32), alpha)
        exchange(s3, r3, n_ss, n_rs, z, in_z)

    def coefficients():
        arrived(s3, r3, n_ss, n_rs, z, in_z)
        for h in range(HEADS):
            al_send[h, 0:8] = r3[:, h, :]
            al_send[h, 8:16] = r3[:, HEADS, :]
        al_all[0] = al_send[r // 2]
        for d in ORDER[:0:-1]:
            to = hop(r, d, RN)
            send(al_send.at[to // 2], al_all.at[8 - d], o_ss.at[d], o_rs.at[8 - d], in_rel(to))

    stage_own(0)
    score, iota_n = scores()
    rows_to_group()
    stage_own(1)
    y_send(3)
    stage_own(7)
    y_send(5)
    scores_along_z()
    stage_near(0)
    stage_own(2)
    stage_own(6)
    y_send(4)
    stage_near(1)
    softmax()
    stage_near(7)
    softmax_rest()
    stage_own(3)
    stage_own(5)
    stage_near(2)
    stage_own(4)
    stage_near(6)
    stage_far(0)
    stage_far(1)
    stage_far(7)
    stage_near(3)
    hot_wait()
    for i in range(G):
        hot(i)
    stage_pick(0)
    stage_near(5)
    stage_far(2)
    stage_pick(1)
    coefficients()
    stage_pick(7)
    stage_near(4)
    stage_far(6)
    stage_pick(2)
    stage_far(3)
    stage_pick(6)
    stage_far(5)
    stage_pick(3)
    stage_far(4)
    stage_pick(5)
    stage_pick(4)

    for d in range(1, 8):
        copy(al_send.at[0], al_all.at[d], o_ss.at[d], o_rs.at[d], in_rel(hop(r, d, RN))).wait_recv()

    def part(zt):
        acc = jnp.zeros((N, CB), F32)
        for j in range(0, RN, 2):
            both = []
            for jj in (j, j + 1):
                alpha = al_all[jj, pl.ds(zt, 1), :]
                target = al_all[jj, pl.ds(zt + 8, 1), :]
                both.append(jnp.where(target == iota_n.astype(F32), alpha, 0.0).astype(BF))
            acc = acc + dot(jnp.concatenate(both, axis=1), picked[zt, j * 128 : j * 128 + 256, :])
        return acc

    half = N // 2

    spans = ((0, half), (half, half))

    def ring(way, kind):
        to = hop(z, (1 if way == 0 else -1) * (1, 1, 2, 1, 2, 2)[kind], ZN)
        shared, alone = spans[way], spans[1 - way]
        rows = pl.ds(*(alone, shared, shared, (0, N), alone, shared)[kind])
        slot = (0, 0, 1, 2, 3, 3)[kind]
        return copy(
            zs.at[way, slot, rows], zr.at[way, slot, rows], z_ss.at[way, kind], z_rs.at[way, kind], in_z(to)
        )

    def ring_send(way, kind):
        c = ring(way, kind)
        c.start()
        sent.append(c)

    before = tuple(sent)
    sent.clear()
    for way, sign in ((0, 1), (1, -1)):
        zs[way, 0] = part(hop(z, 3 * sign, ZN)).astype(BF)
        ring_send(way, 0)
        ring_send(way, 1)
    far = part(hop(z, 4, ZN)).astype(BF)
    for way in (0, 1):
        rows = slice(half * way, half * (way + 1))
        zs[way, 1, rows] = far[rows]
        ring_send(way, 2)
    for way, sign in ((0, 1), (1, -1)):
        zs[way, 2] = part(hop(z, sign, ZN)).astype(BF)
        ring_send(way, 3)
    mine = [part(hop(z, 2 * sign, ZN)) for sign in (1, -1)]
    for c in before:
        c.wait_send()
    for way in (0, 1):
        ring(way, 0).wait_recv()
        rows = slice(half * (1 - way), half * (2 - way))
        zs[way, 3, rows] = (mine[way][rows] + zr[way, 0, rows].astype(F32)).astype(BF)
        ring_send(way, 4)
    own = part(z)
    for way in (0, 1):
        ring(way, 1).wait_recv()
        ring(way, 2).wait_recv()
        rows = slice(half * way, half * (way + 1))
        zs[way, 3, rows] = (mine[way][rows] + zr[way, 0, rows].astype(F32) + zr[way, 1, rows].astype(F32)).astype(BF)
        ring_send(way, 5)
    for way in (0, 1):
        ring(way, 3).wait_recv()
        own = own + zr[way, 2].astype(F32)
    for way in (0, 1):
        ring(way, 4).wait_recv()
    for way in (0, 1):
        ring(way, 5).wait_recv()
        own = own + zr[way, 3].astype(F32)
    out_ref[...] = own.astype(BF)
    for c in sent:
        c.wait_send()


def on_device(node_feats, rel_weight, att_src, att_dst, src_row, dst_row):
    src = src_row.reshape(64, 16).T
    dst = dst_row.reshape(64, 16).T
    vmem = pl.BlockSpec(memory_space=pltpu.VMEM)
    hbm = pl.BlockSpec(memory_space=pltpu.HBM)
    tile8 = pltpu.VMEM((8, 8, 128), F32)
    dma = pltpu.SemaphoreType.DMA
    return pl.pallas_call(
        kernel,
        out_shape=pltpu.VMEM((N, CB), BF),
        in_specs=[hbm] * 6,
        out_specs=vmem,
        scratch_shapes=[
            pltpu.VMEM((N, D), BF),
            pltpu.VMEM((D, D), BF),
            pltpu.VMEM((1, D), F32), pltpu.VMEM((1, D), F32),
            pltpu.VMEM((16, 64), jnp.int32), pltpu.VMEM((16, 64), jnp.int32),
            pltpu.VMEM((8, 128), jnp.int32), pltpu.VMEM((8, 128), jnp.int32),
            pltpu.VMEM((64, 128), F32),
            pltpu.VMEM((RN, N, CB), BF),
            pltpu.VMEM((G, RN, N, CB), BF),
            pltpu.VMEM((RN, G, 128, N), BF),
            pltpu.VMEM((ZN, D, CB), BF),
            tile8, tile8,
            pltpu.VMEM((8, 128), F32),
            tile8,
            tile8, tile8, tile8, tile8, tile8, tile8,
            pltpu.VMEM((HEADS, 16, 128), F32),
            pltpu.VMEM((RN, 16, 128), F32),
            pltpu.VMEM((N, 128), F32),
            pltpu.VMEM((ZN, N, 128), BF),
            tile8,
            pltpu.VMEM((2, 4, N, CB), BF),
            pltpu.VMEM((2, 4, N, CB), BF),
            dma((6,)), dma((4,)),
            dma((8,)), dma((8,)),
            dma((7, 8)), dma((7, 8)),
            dma((8,)), dma((8,)),
            dma((8,)), dma((8,)),
            dma((8,)), dma((8,)),
            dma((8,)), dma((8,)),
            dma((8,)), dma((8,)),
            dma((8,)), dma((8,)),
            dma((2, 6)), dma((2, 6)),
        ],
        compiler_params=pltpu.CompilerParams(
            collective_id=0, has_side_effects=True, vmem_limit_bytes=62 * 1024 * 1024
        ),
    )(node_feats, rel_weight[0], att_src, att_dst, src, dst)


def solution(mesh):
    placed = (
        P("dom", None),
        P("rel", None, None),
        P("rel", None),
        P("rel", None),
        P("rel", "dom", None, None),
        P("rel", "dom", None, None),
    )
    return jax.shard_map(
        on_device, mesh=mesh, in_specs=placed, out_specs=P("dom", "rel"), check_vma=False
    )
```
